32 devices in a mesh: freq: 8 (over z, y), patch: 4 (over x, core).
Axes of the slice: x: 2, y: 2, z: 4, core: 2. Of those that a mesh axis runs over, the one named last changes fastest.
Arguments:
- pressures: bfloat16 [2, 128, 131072], P(None, 'freq', 'patch'), may hold values from -6 to 6
- templates: bfloat16 [4, 128, 128], replicated, may hold values from -0.5 to 0.5
- panel_map: int32 [1024, 4], P('patch'), may hold values from 0 to 511, as said below
- blend_weights: float32 [1024, 4], P('patch'), may hold values from 0.1 to 1
- pattern_label: int32 [1024], P('patch'), may hold values from 0 to 3
- zone_ids: int32 [128, 1024], P('patch', 'freq'), may hold values from 0 to 7
- zone_gain: float32 [8], replicated, may hold values from 0.5 to 2
- stiffness: float32 [128, 1024], P('patch', 'freq'), may hold values from 0.05 to 0.5
Outputs:
- plate_stress: bfloat16 [1024, 128, 1024], P(None, 'patch', 'freq')
The draws below stay inside these ranges and needn't reach their ends.
Inputs may be any that keep to these rules, and one draw needn't show every extreme that they name: `panel_map`: node blocks of region 0 name only values of 256 or more.
All inputs are finite; a program needn't handle non-finite values.
Results may differ from the reference program's by a relative error of at most 0.0068.
Values may be sent and summed in bfloat16 or wider, within the bound.
A program may use at most 128 MiB of HBM per device.

```python
import math
import jax
import jax.numpy as jnp
from jax import lax

F = 128
NT = 1024
PW = 128
MT = 4
K = 4
NZONE = 8
PB = 256
ROW_DEV = 32
GR = 128
GC = 1024
NB_REG = 256
NBLK = 1024
PANELS = 131072
N_PATCH = 4


def draw_panel_map(key, part):
    positions = jnp.arange(NBLK, dtype=jnp.int32)[:, None]
    lowest = jnp.where(positions < NB_REG, PB, 0).astype(jnp.int32)
    raw_values = jax.random.randint(key, (NBLK, K), 0, 2 * PB, dtype=jnp.int32)
    return (lowest + raw_values % (2 * PB - lowest)).astype(jnp.int32)


def with_ends(values, rng, least, top_value):
    extent = values.shape
    index_at = [jax.random.randint(jax.random.fold_in(rng, axis), (), 0, extent[axis]) for axis in range(len(extent))]
    values = values.at[tuple(index_at)].set(least)
    longest = extent.index(max(extent))
    index_at[longest] = (index_at[longest] + 1) % extent[longest]
    return values.at[tuple(index_at)].set(top_value)


def steps_of(key, dims, pieces, low, top_value):
    factor_of = 1.0
    for axis_at, parts in pieces:
        heights = jax.random.uniform(jax.random.fold_in(jax.random.fold_in(key, 6), axis_at), (parts,), jnp.float32, low / len(pieces), top_value / len(pieces))
        factor_of = factor_of * jnp.repeat(jnp.exp(heights), dims[axis_at] // parts).reshape((-1,) + (1,) * (len(dims) - 1 - axis_at))
    return factor_of


def noise(key, shape, spread, limit, split=(), kind=jnp.bfloat16):
    factor_of = steps_of(key, shape, split, -0.22, 0.18) if split else 1.0
    values = jax.random.normal(key, shape, jnp.float32) * spread * factor_of
    return jnp.minimum(jnp.maximum(values, -limit), limit).astype(kind)


def setup_inputs(seed: int = 0) -> dict:
    key_list = jax.random.split(jax.random.key(seed), 9)
    pressures = noise(key_list[0], (2, F, PANELS), 1.0, 6.0, ((1, 8), (2, 4)))
    templates = noise(key_list[1], (MT, PW, PW), PW ** -0.5, 0.5)
    panel_map = draw_panel_map(jax.random.fold_in(key_list[8], 71), 0)
    blend_weights = jnp.clip(0.1 + 0.9 * jax.random.uniform(key_list[3], (NBLK, K), jnp.float32) ** steps_of(key_list[3], (NBLK, K), ((0, 4),), -0.2, 0.2), 0.1, 1.0)
    pattern_label = with_ends(jax.random.randint(key_list[4], (NBLK,), 0, MT), jax.random.fold_in(key_list[4], 1), 0, MT - 1).astype(jnp.int32)
    zone_ids = with_ends(jax.random.randint(key_list[5], (GR, GC), 0, NZONE), jax.random.fold_in(key_list[5], 1), 0, NZONE - 1).astype(jnp.int32)
    zone_gain = jnp.clip(jnp.exp(jax.random.uniform(key_list[6], (NZONE,), jnp.float32, math.log(0.5), math.log(2.0))), 0.5, 2.0)
    stiffness = jnp.clip(jnp.exp(math.log(0.5) - 2.3025851 * jax.random.uniform(key_list[7], (GR, GC), jnp.float32) ** steps_of(key_list[7], (GR, GC), ((0, 4), (1, 8)), -0.2, 0.2)), 0.05, 0.5)
    return {"pressures": pressures, "templates": templates, "panel_map": panel_map, "blend_weights": blend_weights, "pattern_label": pattern_label, "zone_ids": zone_ids, "zone_gain": zone_gain, "stiffness": stiffness}


def fourier_matrix(increment_total, nfreq):
    clock_moments = jnp.arange(increment_total, dtype=jnp.int32)
    sinusoid_components = jnp.arange(1, nfreq + 1, dtype=jnp.int32)
    cycle_offsets_radians = clock_moments[:, None] * sinusoid_components[None, :] % increment_total
    angles = cycle_offsets_radians.astype(jnp.float32) * (2.0 * math.pi / increment_total)
    return jnp.concatenate([jnp.cos(angles), -jnp.sin(angles)], axis=1).astype(jnp.bfloat16)

def build_histories(spectra, increment_total):
    nfreq = spectra.shape[1]
    row_count = spectra.shape[2]
    col_count = spectra.shape[3]
    table = fourier_matrix(increment_total, nfreq)
    piled_arrays = spectra.reshape(2 * nfreq, row_count * col_count)
    load_series = jnp.dot(table, piled_arrays, preferred_element_type=jnp.float32)
    load_series = load_series * (1.0 / math.sqrt(nfreq))
    return load_series.reshape(increment_total, row_count, col_count).astype(jnp.bfloat16)

def blend_blocks(lookup_table, indices, weights):
    running = jnp.zeros((lookup_table.shape[0], indices.shape[0], lookup_table.shape[2]), jnp.float32)
    for position_index in range(indices.shape[1]):
        picked = jnp.take(lookup_table, indices[:, position_index], axis=1).astype(jnp.float32)
        running = running + weights[:, position_index][None, :, None] * picked
    return running.astype(jnp.bfloat16)

def apply_templates(blended, pattern_label, templates):
    count = templates.shape[0]
    width = templates.shape[1]
    piled_arrays = jnp.transpose(templates, (1, 0, 2)).reshape(width, count * width)
    flat = blended.reshape(-1, width)
    products = jnp.dot(flat, piled_arrays, preferred_element_type=jnp.float32)
    products = products.reshape(blended.shape[0], blended.shape[1], count, width)
    chosen = pattern_label[:, None] == jnp.arange(count, dtype=jnp.int32)[None, :]
    picked = lax.optimization_barrier(jnp.sum(jnp.where(chosen[None, :, :, None], products, jnp.float32(0.0)), axis=2))
    return picked.astype(jnp.bfloat16)

def stencil_stress(padded_series, zone_ids, zone_gain, stiffness):
    centre = padded_series[:, 1:-1, 1:-1].astype(jnp.float32)
    beside_all = padded_series[:, :-2, 1:-1].astype(jnp.float32) + padded_series[:, 2:, 1:-1].astype(jnp.float32)
    beside_all = beside_all + padded_series[:, 1:-1, :-2].astype(jnp.float32) + padded_series[:, 1:-1, 2:].astype(jnp.float32)
    zones = jnp.arange(zone_gain.shape[0], dtype=jnp.int32)
    gain_field = lax.optimization_barrier(jnp.sum(jnp.where(zone_ids[:, :, None] == zones[None, None, :], zone_gain[None, None, :], jnp.float32(0.0)), axis=2))
    result = gain_field[None] * (centre + stiffness[None] * (4.0 * centre - beside_all))
    return result.astype(jnp.bfloat16)

def reference(pressures, templates, panel_map, blend_weights, pattern_label, zone_ids, zone_gain, stiffness):
    lookup_table = pressures.reshape(2 * F, N_PATCH * PB, PW)
    maps = panel_map.reshape(N_PATCH, NB_REG, K)
    weights = blend_weights.reshape(N_PATCH, NB_REG, K)
    chosen_ids = pattern_label.reshape(N_PATCH, NB_REG)
    sectors = jnp.arange(N_PATCH, dtype=jnp.int32)

    def map_region(inputs):
        region, indices, region_weights, region_ids = inputs
        global_ids = (region - 1) * PB + indices
        blended = blend_blocks(lookup_table, global_ids, region_weights)
        return apply_templates(blended, region_ids, templates)
    mapped = lax.map(map_region, (sectors, maps, weights, chosen_ids))
    mapped = mapped.reshape(N_PATCH, 2, F, ROW_DEV, GC)
    node_spectra = jnp.transpose(mapped, (1, 2, 0, 3, 4)).reshape(2, F, GR, GC)
    padded = jnp.pad(node_spectra, ((0, 0), (0, 0), (1, 1), (1, 1)))

    def stress_region(region):
        start = (region * ROW_DEV).astype(jnp.int32)
        spectra_rows = lax.dynamic_slice_in_dim(padded, start, ROW_DEV + 2, 2)
        load_series = build_histories(spectra_rows, NT)
        zone_rows = lax.dynamic_slice_in_dim(zone_ids, start, ROW_DEV, 0)
        stiff_rows = lax.dynamic_slice_in_dim(stiffness, start, ROW_DEV, 0)
        return stencil_stress(load_series, zone_rows, zone_gain, stiff_rows)
    stressed_plate = lax.map(stress_region, sectors)
    return jnp.transpose(stressed_plate, (1, 0, 2, 3)).reshape(NT, GR, GC)
```

```python
import functools
import math

import jax
import jax.numpy as jnp
from jax import lax
from jax.experimental import pallas as pl
from jax.experimental.pallas import tpu as pltpu
from jax.sharding import PartitionSpec as P

NT = 1024
PW = 128
GROUPS = 3
VMEM_LIMIT = 63 * 1024 * 1024
BF16 = jnp.bfloat16
F32 = jnp.float32


def row_cuts(rows):
    inner = rows - 2
    return [1 + inner * n // GROUPS for n in range(GROUPS + 1)]


def fourier_factors(nt, fine, nfreq, fl, whole):
    step = lax.broadcasted_iota(jnp.int32, (fine, 2 * nfreq), 0)
    order = lax.broadcasted_iota(jnp.int32, (fine, 2 * nfreq), 1)
    if whole:
        real, freq = order < nfreq, order % nfreq
    else:
        real, freq = order // fl % 2 == 0, order // (2 * fl) * fl + order % fl

    def angles(clock):
        turns = clock * (freq + 1) % nt
        return turns.astype(F32) * (2.0 * math.pi / nt)

    coarse, small = angles(step * fine), angles(step)
    cosine, sine = jnp.cos(coarse), jnp.sin(coarse)
    return (jnp.where(real, cosine, -sine), jnp.where(real, sine, cosine),
            jnp.cos(small), jnp.sin(small))


def exchange_kernel(rows, groups, owners, patches, scale, map_ref, weight_ref, label_ref, gain_ref, own_ref,
                    templates_ref, zone_ref, stiff_ref, out_ref, dft_ref,
                    blended, spectra, load, coefs, coef_ref, stacked, factors, local_sem, press_sem, edge_sem,
                    coef_sem, column_sem, *tables):
    pieces, cf, width = own_ref.shape
    kinds = templates_ref.shape[0]
    me, patch = lax.axis_index("freq"), lax.axis_index("patch")
    has_prev, has_next = patch > 0, patch < patches - 1
    lane = lax.broadcasted_iota(jnp.int32, (groups, cf, PW), 2)
    empty = jnp.zeros((1, cf, PW), F32)
    cuts = row_cuts(rows)
    far_first = sorted(range(1, owners), key=lambda k: -min(k, owners - k))

    def partner(k):
        return lax.rem(me + k, owners)

    def source(k):
        return lax.rem(me + owners - k, owners)

    def remote(src, dst, sems, at, **device):
        return pltpu.make_async_remote_copy(
            src_ref=src, dst_ref=dst, send_sem=sems.at[(0,) + at], recv_sem=sems.at[(1,) + at],
            device_id=device, device_id_type=pl.DeviceIdType.MESH)

    def pressure_copy(p):
        return remote(own_ref.at[p], tables[p].at[:, pl.ds(0, width)], press_sem, (p,),
                      patch=patch + 1)

    def own_copy(p):
        return pltpu.make_async_copy(
            own_ref.at[p], tables[p].at[:, pl.ds(width, width)], local_sem.at[p])

    def down_copy(p):
        return remote(spectra.at[p, rows], spectra.at[p, 0], edge_sem, (p, 0), patch=patch + 1)

    def up_copy(p):
        return remote(spectra.at[p, 1], spectra.at[p, rows + 1], edge_sem, (p, 1),
                      patch=patch - 1)

    def coef_copy(k, slot):
        return remote(coef_ref, coefs.at[slot], coef_sem, (k,), freq=partner(k))

    def inner_copy(p, n, k, slot):
        part = pl.ds(cuts[n] - 1, cuts[n + 1] - cuts[n])
        return remote(load.at[partner(k), p, part], out_ref.at[slot, p, part], column_sem,
                      (p * GROUPS + n, k), freq=partner(k))

    def outer_copy(k, slot):
        part = pl.ds(rows - 2, 2)
        return remote(load.at[partner(k), :, part], out_ref.at[slot, :, part], column_sem,
                      (pieces * GROUPS, k), freq=partner(k))

    def keep_copy():
        return pltpu.make_async_copy(load.at[me], out_ref.at[me], local_sem.at[pieces])

    barrier = pltpu.get_barrier_semaphore()
    for k in range(1, owners):
        pl.semaphore_signal(barrier, inc=1, device_id={"freq": partner(k)},
                            device_id_type=pl.DeviceIdType.MESH)

    @pl.when(has_prev)
    def _():
        pl.semaphore_signal(barrier, inc=1, device_id={"patch": patch - 1},
                            device_id_type=pl.DeviceIdType.MESH)

    @pl.when(has_next)
    def _():
        pl.semaphore_signal(barrier, inc=1, device_id={"patch": patch + 1},
                            device_id_type=pl.DeviceIdType.MESH)

    for p in range(pieces):
        own_copy(p).start()
    gain = jnp.zeros(zone_ref.shape, F32)
    for zone in range(gain_ref.shape[0]):
        gain = jnp.where(zone_ref[...] == zone, gain_ref[zone], gain)
    gain = gain * scale
    coef_ref[0] = gain * (1.0 + 4.0 * stiff_ref[...])
    coef_ref[1] = gain * stiff_ref[...]
    pl.semaphore_wait(
        barrier, owners - 1 + has_prev.astype(jnp.int32) + has_next.astype(jnp.int32))

    @pl.when(has_next)
    def _():
        pressure_copy(0).start()

    for k in range(1, owners):
        coef_copy(k, me).start()
    coefs[me] = coef_ref[...]
    for kind in range(kinds):
        stacked[:, kind * PW:(kind + 1) * PW] = templates_ref[kind]

    @pl.when(jnp.logical_not(has_prev))
    def _():
        for p in range(pieces):
            tables[p][:, :width] = jnp.zeros((cf, width), BF16)
            spectra[p, 0] = jnp.zeros((groups, cf, PW), BF16)

    @pl.when(jnp.logical_not(has_next))
    def _():
        for p in range(pieces):
            spectra[p, rows + 1] = jnp.zeros((groups, cf, PW), BF16)

    def blend_row(p, i):
        for g in range(groups):
            total = None
            for j in range(4):
                at = map_ref[j, i * groups + g] * PW
                term = tables[p][:, pl.ds(at, PW)].astype(F32) * weight_ref[j, i * groups + g]
                total = term if total is None else total + term
            blended[i, g] = total.astype(BF16)

    def map_row(p, i):
        flat = blended[i].reshape(groups * cf, PW)
        products = jnp.dot(flat, stacked[...], preferred_element_type=F32)
        for g in range(groups):
            label = jnp.full((1, PW), label_ref[i * groups + g], jnp.int32)
            block = products[g * cf:(g + 1) * cf]
            picked = block[:, :PW]
            for kind in range(1, kinds):
                picked = jnp.where(label == kind, block[:, kind * PW:(kind + 1) * PW], picked)
            spectra[p, i + 1, g] = picked.astype(BF16)

    def stress_row(p, i, at):
        here = spectra[p, i + 1].astype(F32)
        from_left = pltpu.roll(here, 1, 2)
        from_right = pltpu.roll(here, PW - 1, 2)
        left = jnp.where(lane == 0, jnp.concatenate([empty, from_left[:-1]], 0), from_left)
        right = jnp.where(
            lane == PW - 1, jnp.concatenate([from_right[1:], empty], 0), from_right)
        beside = spectra[p, i].astype(F32) + spectra[p, i + 2].astype(F32) + left + right
        centre_gain = coefs[:, 0, i][:, None, :]
        beside_gain = coefs[:, 1, i][:, None, :]
        load[:, p, at] = (centre_gain * here - beside_gain * beside).astype(BF16)

    def inner_stress(p, i):
        stress_row(p, i, i - 1)

    def each(first, last, act, p, unroll):
        def body(i, carry):
            act(p, i)
            return carry
        lax.fori_loop(first, last, body, 0, unroll=unroll)

    for p in range(pieces):
        own_copy(p).wait()

        @pl.when(has_prev)
        def _():
            pressure_copy(p).wait_recv()

        for act in (blend_row, map_row):
            act(p, 0)
            act(p, rows - 1)

        @pl.when(has_prev)
        def _():
            up_copy(p).start()

        @pl.when(has_next)
        def _():
            down_copy(p).start()

        for n in range(GROUPS):
            first = cuts[n] + (n > 0)
            last = min(cuts[n + 1] + 1, rows - 1)
            each(first, last, blend_row, p, 2)
            each(first, last, map_row, p, 3)
            if p == 0 and n == 0:
                for k in range(1, owners):
                    coef_copy(k, source(k)).wait_recv()
            each(cuts[n], cuts[n + 1], inner_stress, p, 2)
            for k in far_first:
                inner_copy(p, n, k, me).start()

        @pl.when(has_next)
        def _():
            pressure_copy(p).wait_send()
            if p + 1 < pieces:
                pressure_copy(p + 1).start()

    for p in range(pieces):
        @pl.when(has_prev)
        def _():
            down_copy(p).wait_recv()

        @pl.when(has_next)
        def _():
            up_copy(p).wait_recv()

        stress_row(p, 0, rows - 2)
        stress_row(p, rows - 1, rows - 1)
    for k in far_first:
        outer_copy(k, me).start()
    keep_copy().start()

    for n, values in enumerate(
            fourier_factors(NT, factors.shape[1], factors.shape[2] // 2, cf * pieces // 2, pieces == 2)):
        factors[n] = values

    def table_rows(n, carry):
        values = (factors[0, pl.ds(n, 1)] * factors[2] - factors[1, pl.ds(n, 1)] * factors[3])
        dft_ref[n] = values.astype(BF16)
        return carry

    lax.fori_loop(0, factors.shape[1], table_rows, 0)

    @pl.when(has_next)
    def _():
        for p in range(pieces):
            down_copy(p).wait_send()

    @pl.when(has_prev)
    def _():
        for p in range(pieces):
            up_copy(p).wait_send()

    for k in range(1, owners):
        coef_copy(k, me).wait_send()
    keep_copy().wait()
    for k in range(1, owners):
        for p in range(pieces):
            for n in range(GROUPS):
                inner_copy(p, n, k, me).wait_send()
                inner_copy(p, n, k, source(k)).wait_recv()
        outer_copy(k, me).wait_send()
        outer_copy(k, source(k)).wait_recv()


def exchange(panel_map, weights, labels, zone_gain, own, templates, zone_ids, stiffness, scale,
             groups, owners, patches):
    rows = zone_ids.shape[0]
    pieces, cf, width = own.shape
    kinds = templates.shape[0]
    depth = owners * pieces * cf
    fine = math.isqrt(NT)
    smem = pl.BlockSpec(memory_space=pltpu.SMEM)
    hbm = pl.BlockSpec(memory_space=pl.ANY)
    vmem = pl.BlockSpec(memory_space=pltpu.VMEM)
    dma = pltpu.SemaphoreType.DMA
    return pl.pallas_call(
        functools.partial(exchange_kernel, rows, groups, owners, patches, scale),
        out_shape=(
            jax.ShapeDtypeStruct((owners, pieces, rows, cf, PW), BF16),
            jax.ShapeDtypeStruct((fine, fine, depth), BF16),
        ),
        in_specs=[smem, smem, smem, smem, hbm, vmem, vmem, vmem],
        out_specs=(hbm, vmem),
        scratch_shapes=[
            pltpu.VMEM((rows, groups, cf, PW), BF16),
            pltpu.VMEM((pieces, rows + 2, groups, cf, PW), BF16),
            pltpu.VMEM((groups, pieces, rows, cf, PW), BF16),
            pltpu.VMEM((owners, 2, rows, PW), F32),
            pltpu.VMEM((2, rows, PW), F32),
            pltpu.VMEM((PW, kinds * PW), BF16),
            pltpu.VMEM((4, fine, depth), F32),
            dma((pieces + 1,)),
            dma((2, pieces)),
            dma((2, pieces, 2)),
            dma((2, owners)),
            dma((2, pieces * GROUPS + 1, owners)),
        ] + [pltpu.VMEM((cf, 2 * width), BF16)] * pieces,
        compiler_params=pltpu.CompilerParams(
            vmem_limit_bytes=VMEM_LIMIT, collective_id=0, has_side_effects=True),
        cost_estimate=pl.CostEstimate(
            flops=2 * own.size * kinds * PW, bytes_accessed=40 * own.size,
            transcendentals=0),
    )(panel_map, weights, labels, zone_gain, own, templates, zone_ids, stiffness)


def history_kernel(rows, pieces, *refs):
    table_ref, load_ref, out_ref, wide = refs
    steps = table_ref.shape[0]
    stride = rows + 1
    for r in range(0, rows, 2):
        sides = []
        for q in (r, r + 1):
            at = q - 1 if 0 < q < rows - 1 else rows - 2 + (q > 0)
            stack = [load_ref[:, piece, at].reshape(-1, PW) for piece in range(pieces)]
            sides.append(stack[0] if pieces == 1 else jnp.concatenate(stack, 0))
        values = jnp.dot(
            table_ref[...], jnp.concatenate(sides, 1), preferred_element_type=F32)
        wide[pl.ds(r, steps, stride=stride), :] = values[:, :PW]
        wide[pl.ds(r + 1, steps, stride=stride), :] = values[:, PW:]
    for t in range(steps):
        out_ref[t] = wide[pl.ds(t * stride, rows), :].astype(BF16)


def histories(table, load):
    nt, depth = table.shape
    pieces, rows = load.shape[1:3]
    steps = 256
    whole = pl.BlockSpec(memory_space=pltpu.VMEM)
    return pl.pallas_call(
        functools.partial(history_kernel, rows, pieces),
        grid=(nt // steps,),
        out_shape=jax.ShapeDtypeStruct((nt, rows, PW), BF16),
        in_specs=[pl.BlockSpec((steps, depth), lambda t: (t, 0)), whole],
        out_specs=pl.BlockSpec((steps, rows, PW), lambda t: (t, 0, 0)),
        scratch_shapes=[pltpu.VMEM(((steps + 1) * (rows + 1), PW), F32)],
        compiler_params=pltpu.CompilerParams(vmem_limit_bytes=VMEM_LIMIT),
        cost_estimate=pl.CostEstimate(
            flops=2 * nt * depth * rows * PW, bytes_accessed=2 * nt * rows * PW,
            transcendentals=0),
    )(table, load)


def shards(
    pressures, templates, panel_map, blend_weights, pattern_label, zone_ids, zone_gain, stiffness
):
    owners = lax.axis_size("freq")
    fl = pressures.shape[1]
    nfreq = fl * owners
    rows, cols = zone_ids.shape
    groups = owners * cols // PW

    pieces = 2 if fl % 16 == 0 else 1
    own = pressures.reshape(pieces, 2 * fl // pieces, pressures.shape[2])
    load, table = exchange(
        panel_map.T, blend_weights.T, pattern_label, zone_gain, own, templates, zone_ids, stiffness,
        1.0 / math.sqrt(nfreq), groups, owners, lax.axis_size("patch"))
    return histories(table.reshape(NT, 2 * nfreq), load)


def solution(mesh):
    placed = (
        P(None, "freq", "patch"),
        P(),
        P("patch", None),
        P("patch", None),
        P("patch"),
        P("patch", "freq"),
        P(),
        P("patch", "freq"),
    )
    return jax.shard_map(
        shards, mesh=mesh, in_specs=placed, out_specs=P(None, "patch", "freq"), check_vma=False
    )
```

```python
import functools
import math

import jax
import jax.numpy as jnp
from jax import lax
from jax.experimental import pallas as pl
from jax.experimental.pallas import tpu as pltpu
from jax.sharding import PartitionSpec as P

NT = 1024
PW = 128
BLOCK = 128
SHARES = (0, 2, 6, 10, 14)
GROUPS = len(SHARES) - 1
VMEM_LIMIT = 40 * 1024 * 1024
FINISH_LIMIT = 16 * 1024 * 1024
BF16 = jnp.bfloat16
F32 = jnp.float32


def row_cuts(rows):
    pairs = (rows - 2) // 2
    return [1 + 2 * (pairs * share // SHARES[-1]) for share in SHARES]


def fourier_factors(nt, fine, nfreq, fl, whole):
    step = lax.broadcasted_iota(jnp.int32, (fine, 2 * nfreq), 0)
    order = lax.broadcasted_iota(jnp.int32, (fine, 2 * nfreq), 1)
    if whole:
        real, freq = order < nfreq, order % nfreq
    else:
        real, freq = order // fl % 2 == 0, order // (2 * fl) * fl + order % fl

    def angles(clock):
        turns = clock * (freq + 1) % nt
        return turns.astype(F32) * (2.0 * math.pi / nt)

    coarse, small = angles(step * fine), angles(step)
    cosine, sine = jnp.cos(coarse), jnp.sin(coarse)
    return (jnp.where(real, cosine, -sine), jnp.where(real, sine, cosine),
            jnp.cos(small), jnp.sin(small))


def exchange_kernel(rows, groups, owners, patches, map_ref, weight_ref, label_ref, own_ref,
                    templates_ref, stiff_ref, wide_ref,
                    blended, spectra, load, arrived, own_stiff, stiffs, bending, stacked, factors, table,
                    local_sem, press_sem, edge_sem, stiff_sem, column_sem, *tables):
    pieces, cf, width = own_ref.shape
    kinds = templates_ref.shape[0]
    me, patch = lax.axis_index("freq"), lax.axis_index("patch")
    has_prev, has_next = patch > 0, patch < patches - 1
    lane = lax.broadcasted_iota(jnp.int32, (groups, cf, PW), 2)
    empty = jnp.zeros((1, cf, PW), F32)
    cuts = row_cuts(rows)
    far_first = sorted(range(1, owners), key=lambda k: -min(k, owners - k))

    def partner(k):
        return lax.rem(me + k, owners)

    def source(k):
        return lax.rem(me + owners - k, owners)

    def remote(src, dst, sems, at, **device):
        return pltpu.make_async_remote_copy(
            src_ref=src, dst_ref=dst, send_sem=sems.at[(0,) + at], recv_sem=sems.at[(1,) + at],
            device_id=device, device_id_type=pl.DeviceIdType.MESH)

    def pressure_copy(p):
        return remote(own_ref.at[p], tables[p].at[:, pl.ds(0, width)], press_sem, (p,),
                      patch=patch + 1)

    def own_copy(p):
        return pltpu.make_async_copy(
            own_ref.at[p], tables[p].at[:, pl.ds(width, width)], local_sem.at[p])

    def down_copy(p):
        return remote(spectra.at[p, rows], spectra.at[p, 0], edge_sem, (p, 0), patch=patch + 1)

    def up_copy(p):
        return remote(spectra.at[p, 1], spectra.at[p, rows + 1], edge_sem, (p, 1),
                      patch=patch - 1)

    def stiff_copy(k, slot):
        return remote(own_stiff, stiffs.at[slot], stiff_sem, (k,), freq=partner(k))

    def inner_copy(p, n, k, slot):
        part = pl.ds(cuts[n] - 1, cuts[n + 1] - cuts[n])
        return remote(load.at[partner(k), p, part], arrived.at[slot, p, part], column_sem,
                      (p * GROUPS + n, k), freq=partner(k))

    def outer_copy(k, slot):
        part = pl.ds(rows - 2, 2)
        return remote(load.at[partner(k), :, part], arrived.at[slot, :, part], column_sem,
                      (pieces * GROUPS, k), freq=partner(k))

    def keep_copy():
        return pltpu.make_async_copy(load.at[me], arrived.at[me], local_sem.at[pieces])

    barrier = pltpu.get_barrier_semaphore()
    for k in range(1, owners):
        pl.semaphore_signal(barrier, inc=1, device_id={"freq": partner(k)},
                            device_id_type=pl.DeviceIdType.MESH)

    @pl.when(has_prev)
    def _():
        pl.semaphore_signal(barrier, inc=1, device_id={"patch": patch - 1},
                            device_id_type=pl.DeviceIdType.MESH)

    @pl.when(has_next)
    def _():
        pl.semaphore_signal(barrier, inc=1, device_id={"patch": patch + 1},
                            device_id_type=pl.DeviceIdType.MESH)

    for p in range(pieces):
        own_copy(p).start()
    own_stiff[...] = stiff_ref[...].astype(BF16)
    pl.semaphore_wait(
        barrier, owners - 1 + has_prev.astype(jnp.int32) + has_next.astype(jnp.int32))

    @pl.when(has_next)
    def _():
        pressure_copy(0).start()

    for k in range(1, owners):
        stiff_copy(k, me).start()
    stiffs[me] = own_stiff[...]
    for kind in range(kinds):
        stacked[:, kind * PW:(kind + 1) * PW] = templates_ref[kind]

    @pl.when(jnp.logical_not(has_prev))
    def _():
        for p in range(pieces):
            tables[p][:, :width] = jnp.zeros((cf, width), BF16)
            spectra[p, 0] = jnp.zeros((groups, cf, PW), BF16)

    @pl.when(jnp.logical_not(has_next))
    def _():
        for p in range(pieces):
            spectra[p, rows + 1] = jnp.zeros((groups, cf, PW), BF16)

    def blend_row(p, i):
        for g in range(groups):
            total = None
            for j in range(4):
                at = map_ref[j, i * groups + g] * PW
                term = tables[p][:, pl.ds(at, PW)].astype(F32) * weight_ref[j, i * groups + g]
                total = term if total is None else total + term
            blended[i, g] = total.astype(BF16)

    def map_row(p, i):
        flat = blended[i].reshape(groups * cf, PW)
        products = jnp.dot(flat, stacked[...], preferred_element_type=F32)
        for g in range(groups):
            label = jnp.full((1, PW), label_ref[i * groups + g], jnp.int32)
            block = products[g * cf:(g + 1) * cf]
            picked = block[:, :PW]
            for kind in range(1, kinds):
                picked = jnp.where(label == kind, block[:, kind * PW:(kind + 1) * PW], picked)
            spectra[p, i + 1, g] = picked.astype(BF16)

    def stress_row(p, i, at):
        here = spectra[p, i + 1].astype(F32)
        from_left = pltpu.roll(here, 1, 2)
        from_right = pltpu.roll(here, PW - 1, 2)
        left = jnp.where(lane == 0, jnp.concatenate([empty, from_left[:-1]], 0), from_left)
        right = jnp.where(
            lane == PW - 1, jnp.concatenate([from_right[1:], empty], 0), from_right)
        beside = spectra[p, i].astype(F32) + spectra[p, i + 2].astype(F32) + left + right
        load[:, p, at] = (here + bending[:, i][:, None, :] * (4.0 * here - beside)).astype(BF16)

    def inner_stress(p, i):
        stress_row(p, i, i - 1)

    def each(first, last, act, p, unroll):
        def body(i, carry):
            act(p, i)
            return carry
        lax.fori_loop(first, last, body, 0, unroll=unroll)

    for p in range(pieces):
        own_copy(p).wait()

        @pl.when(has_prev)
        def _():
            pressure_copy(p).wait_recv()

        for act in (blend_row, map_row):
            act(p, 0)
            act(p, rows - 1)

        @pl.when(has_prev)
        def _():
            up_copy(p).start()

        @pl.when(has_next)
        def _():
            down_copy(p).start()

        for n in range(GROUPS):
            first = cuts[n] + (n > 0)
            last = min(cuts[n + 1] + 1, rows - 1)
            each(first, last, blend_row, p, 2)
            each(first, last, map_row, p, 3)
            if p == 0 and n == 0:
                for k in range(1, owners):
                    stiff_copy(k, source(k)).wait_recv()
                bending[...] = stiffs[...].astype(F32)
            each(cuts[n], cuts[n + 1], inner_stress, p, 2)
            for k in far_first:
                inner_copy(p, n, k, me).start()

        @pl.when(has_next)
        def _():
            pressure_copy(p).wait_send()
            if p + 1 < pieces:
                pressure_copy(p + 1).start()

    for n, values in enumerate(
            fourier_factors(NT, factors.shape[1], factors.shape[2] // 2, cf * pieces // 2, pieces == 2)):
        factors[n] = values

    def table_rows(n, carry):
        values = (factors[0, pl.ds(n, 1)] * factors[2] - factors[1, pl.ds(n, 1)] * factors[3])
        table[n] = values.astype(BF16)
        return carry

    lax.fori_loop(0, factors.shape[1], table_rows, 0)

    for p in range(pieces):
        @pl.when(has_prev)
        def _():
            down_copy(p).wait_recv()

        @pl.when(has_next)
        def _():
            up_copy(p).wait_recv()

        stress_row(p, 0, rows - 2)
        stress_row(p, rows - 1, rows - 1)
    for k in far_first:
        outer_copy(k, me).start()
    keep_copy().start()

    def history_pair(q, row, step):
        sides = []
        for at in (q, q + 1):
            stack = [arrived[:, p, at].reshape(-1, PW) for p in range(pieces)]
            sides.append(stack[0] if pieces == 1 else jnp.concatenate(stack, 0))
        sides = jnp.concatenate(sides, 1)
        depth = sides.shape[0]
        per = 2 * BLOCK // table.shape[1]
        for n in range(NT // (2 * BLOCK)):
            part = table[n * per:(n + 1) * per].reshape(2 * BLOCK, depth)
            values = jnp.dot(part, sides, preferred_element_type=F32)
            for h in range(2):
                for side in range(2):
                    wide_ref[2 * n + h, pl.ds(row + side * step, BLOCK, stride=rows + 1), :] = (
                        values[h * BLOCK:(h + 1) * BLOCK, side * PW:(side + 1) * PW])

    keep_copy().wait()
    for n in range(GROUPS):
        for k in range(1, owners):
            for p in range(pieces):
                inner_copy(p, n, k, source(k)).wait_recv()

        def inner_pair(m, carry):
            q = cuts[n] - 1 + 2 * m
            history_pair(q, q + 1, 1)
            return carry

        lax.fori_loop(0, (cuts[n + 1] - cuts[n]) // 2, inner_pair, 0)

    for k in range(1, owners):
        outer_copy(k, source(k)).wait_recv()
    history_pair(rows - 2, 0, rows - 1)

    @pl.when(has_next)
    def _():
        for p in range(pieces):
            down_copy(p).wait_send()

    @pl.when(has_prev)
    def _():
        for p in range(pieces):
            up_copy(p).wait_send()

    for k in range(1, owners):
        stiff_copy(k, me).wait_send()
        for p in range(pieces):
            for n in range(GROUPS):
                inner_copy(p, n, k, me).wait_send()
        outer_copy(k, me).wait_send()


def exchange(panel_map, weights, labels, own, templates, stiffness, groups, owners, patches):
    rows = stiffness.shape[0]
    pieces, cf, width = own.shape
    kinds = templates.shape[0]
    depth = owners * pieces * cf
    fine = math.isqrt(NT)
    smem = pl.BlockSpec(memory_space=pltpu.SMEM)
    hbm = pl.BlockSpec(memory_space=pl.ANY)
    vmem = pl.BlockSpec(memory_space=pltpu.VMEM)
    dma = pltpu.SemaphoreType.DMA
    return pl.pallas_call(
        functools.partial(exchange_kernel, rows, groups, owners, patches),
        out_shape=pltpu.VMEM((NT // BLOCK, BLOCK * (rows + 1), PW), F32),
        in_specs=[smem, smem, smem, hbm, vmem, vmem],
        out_specs=vmem,
        scratch_shapes=[
            pltpu.VMEM((rows, groups, cf, PW), BF16),
            pltpu.VMEM((pieces, rows + 2, groups, cf, PW), BF16),
            pltpu.VMEM((groups, pieces, rows, cf, PW), BF16),
            pltpu.VMEM((owners, pieces, rows, cf, PW), BF16),
            pltpu.VMEM((rows, PW), BF16),
            pltpu.VMEM((owners, rows, PW), BF16),
            pltpu.VMEM((owners, rows, PW), F32),
            pltpu.VMEM((PW, kinds * PW), BF16),
            pltpu.VMEM((4, fine, depth), F32),
            pltpu.VMEM((fine, fine, depth), BF16),
            dma((pieces + 1,)),
            dma((2, pieces)),
            dma((2, pieces, 2)),
            dma((2, owners)),
            dma((2, pieces * GROUPS + 1, owners)),
        ] + [pltpu.VMEM((cf, 2 * width), BF16)] * pieces,
        compiler_params=pltpu.CompilerParams(
            vmem_limit_bytes=VMEM_LIMIT, collective_id=0, has_side_effects=True),
        cost_estimate=pl.CostEstimate(
            flops=2 * own.size * kinds * PW + 2 * NT * depth * rows * PW,
            bytes_accessed=40 * own.size, transcendentals=0),
    )(panel_map, weights, labels, own, templates, stiffness)


def finish_kernel(scale, gain_ref, zone_ref, wide_ref, out_ref):
    rows = zone_ref.shape[0]
    gain = jnp.zeros(zone_ref.shape, F32)
    for zone in range(gain_ref.shape[0]):
        gain = jnp.where(zone_ref[...] == zone, gain_ref[zone], gain)
    gain = gain * scale
    block = pl.program_id(0)
    for t in range(BLOCK):
        values = wide_ref[block, pl.ds(t * (rows + 1), rows), :]
        out_ref[t] = (values * gain).astype(BF16)


def finish(wide, zone_gain, zone_ids, scale):
    rows = zone_ids.shape[0]
    return pl.pallas_call(
        functools.partial(finish_kernel, scale),
        grid=(NT // BLOCK,),
        out_shape=jax.ShapeDtypeStruct((NT, rows, PW), BF16),
        in_specs=[pl.BlockSpec(memory_space=pltpu.SMEM), pl.BlockSpec(memory_space=pltpu.VMEM),
                  pl.BlockSpec(memory_space=pltpu.VMEM)],
        out_specs=pl.BlockSpec((BLOCK, rows, PW), lambda t: (t, 0, 0)),
        compiler_params=pltpu.CompilerParams(vmem_limit_bytes=FINISH_LIMIT),
        cost_estimate=pl.CostEstimate(
            flops=NT * rows * PW, bytes_accessed=2 * NT * rows * PW, transcendentals=0),
    )(zone_gain, zone_ids, pltpu.with_memory_space_constraint(wide, pltpu.VMEM))


def shards(
    pressures, templates, panel_map, blend_weights, pattern_label, zone_ids, zone_gain, stiffness
):
    owners = lax.axis_size("freq")
    fl = pressures.shape[1]
    nfreq = fl * owners
    rows, cols = zone_ids.shape
    groups = owners * cols // PW

    pieces = 2 if fl % 16 == 0 else 1
    own = pressures.reshape(pieces, 2 * fl // pieces, pressures.shape[2])
    wide = exchange(
        panel_map.T, blend_weights.T, pattern_label, own, templates, stiffness, groups, owners,
        lax.axis_size("patch"))
    return finish(wide, zone_gain, zone_ids, 1.0 / math.sqrt(nfreq))


def solution(mesh):
    placed = (
        P(None, "freq", "patch"),
        P(),
        P("patch", None),
        P("patch", None),
        P("patch"),
        P("patch", "freq"),
        P(),
        P("patch", "freq"),
    )
    return jax.shard_map(
        shards, mesh=mesh, in_specs=placed, out_specs=P(None, "patch", "freq"), check_vma=False
    )
```

```python
import functools
import math

import jax
import jax.numpy as jnp
from jax import lax
from jax.experimental import pallas as pl
from jax.experimental.pallas import tpu as pltpu
from jax.sharding import PartitionSpec as P

NT = 1024
PW = 128
BLOCK = 128
DEEP = 8
FIRST_SHARES = (0, 2, 7, 15)
LAST_SHARES = (0, 7, 15)
VMEM_LIMIT = 40 * 1024 * 1024
FINISH_LIMIT = 16 * 1024 * 1024
BF16 = jnp.bfloat16
F32 = jnp.float32


def row_cuts(rows, shares):
    pairs = (rows - 2) // 2
    return [1 + 2 * (pairs * share // shares[-1]) for share in shares]


def fourier_factors(nt, fine, nfreq, fl, whole):
    step = lax.broadcasted_iota(jnp.int32, (fine, 2 * nfreq), 0)
    order = lax.broadcasted_iota(jnp.int32, (fine, 2 * nfreq), 1)
    if whole:
        real, freq = order < nfreq, order % nfreq
    else:
        real, freq = order // fl % 2 == 0, order // (2 * fl) * fl + order % fl

    def angles(clock):
        turns = clock * (freq + 1) % nt
        return turns.astype(F32) * (2.0 * math.pi / nt)

    coarse, small = angles(step * fine), angles(step)
    cosine, sine = jnp.cos(coarse), jnp.sin(coarse)
    return (jnp.where(real, cosine, -sine), jnp.where(real, sine, cosine),
            jnp.cos(small), jnp.sin(small))


def exchange_kernel(rows, groups, owners, patches, map_ref, weight_ref, label_ref, own_ref,
                    templates_ref, stiff_ref, wide_ref,
                    blended, spectra, load, arrived, own_stiff, stiffs, bending, stacked, factors, table,
                    local_sem, press_sem, edge_sem, stiff_sem, column_sem, *tables):
    pieces, cf, width = own_ref.shape
    kinds = templates_ref.shape[0]
    me, patch = lax.axis_index("freq"), lax.axis_index("patch")
    has_prev, has_next = patch > 0, patch < patches - 1
    lane = lax.broadcasted_iota(jnp.int32, (groups, cf, PW), 2)
    empty = jnp.zeros((1, cf, PW), F32)
    cuts = [row_cuts(rows, LAST_SHARES if p == pieces - 1 else FIRST_SHARES) for p in range(pieces)]
    offsets = [sum(len(c) - 1 for c in cuts[:p]) for p in range(pieces + 1)]
    far_first = sorted(range(1, owners), key=lambda k: -min(k, owners - k))

    def partner(k):
        return lax.rem(me + k, owners)

    def source(k):
        return lax.rem(me + owners - k, owners)

    def remote(src, dst, sems, at, **device):
        return pltpu.make_async_remote_copy(
            src_ref=src, dst_ref=dst, send_sem=sems.at[(0,) + at], recv_sem=sems.at[(1,) + at],
            device_id=device, device_id_type=pl.DeviceIdType.MESH)

    def pressure_copy(p):
        return remote(own_ref.at[p], tables[p].at[:, pl.ds(0, width)], press_sem, (p,),
                      patch=patch + 1)

    def own_copy(p):
        return pltpu.make_async_copy(
            own_ref.at[p], tables[p].at[:, pl.ds(width, width)], local_sem.at[p])

    def down_copy(p):
        return remote(spectra.at[p, rows], spectra.at[p, 0], edge_sem, (p, 0), patch=patch + 1)

    def up_copy(p):
        return remote(spectra.at[p, 1], spectra.at[p, rows + 1], edge_sem, (p, 1),
                      patch=patch - 1)

    def stiff_copy(k, slot):
        return remote(own_stiff, stiffs.at[slot], stiff_sem, (k,), freq=partner(k))

    def column_copy(p, n, k, slot):
        part = pl.ds(cuts[p][n] - 1, cuts[p][n + 1] - cuts[p][n])
        return remote(load.at[partner(k), p, part], arrived.at[slot, p, part], column_sem,
                      (offsets[p] + n, k), freq=partner(k))

    def edge_copy(k, slot):
        part = pl.ds(rows - 2, 2)
        return remote(load.at[partner(k), :, part], arrived.at[slot, :, part], column_sem,
                      (offsets[pieces], k), freq=partner(k))

    sent = [(p, n) for p in range(pieces) for n in range(len(cuts[p]) - 1)]

    def keep_copy():
        return pltpu.make_async_copy(load.at[me], arrived.at[me], local_sem.at[pieces])

    barrier = pltpu.get_barrier_semaphore()
    for k in range(1, owners):
        pl.semaphore_signal(barrier, inc=1, device_id={"freq": partner(k)},
                            device_id_type=pl.DeviceIdType.MESH)

    @pl.when(has_prev)
    def _():
        pl.semaphore_signal(barrier, inc=1, device_id={"patch": patch - 1},
                            device_id_type=pl.DeviceIdType.MESH)

    @pl.when(has_next)
    def _():
        pl.semaphore_signal(barrier, inc=1, device_id={"patch": patch + 1},
                            device_id_type=pl.DeviceIdType.MESH)

    for p in range(pieces):
        own_copy(p).start()
    own_stiff[...] = stiff_ref[...].astype(BF16)
    pl.semaphore_wait(
        barrier, owners - 1 + has_prev.astype(jnp.int32) + has_next.astype(jnp.int32))

    @pl.when(has_next)
    def _():
        pressure_copy(0).start()

    for k in range(1, owners):
        stiff_copy(k, me).start()
    stiffs[me] = own_stiff[...]
    for kind in range(kinds):
        stacked[:, kind * PW:(kind + 1) * PW] = templates_ref[kind]

    @pl.when(jnp.logical_not(has_prev))
    def _():
        for p in range(pieces):
            tables[p][:, :width] = jnp.zeros((cf, width), BF16)
            spectra[p, 0] = jnp.zeros((groups, cf, PW), BF16)

    @pl.when(jnp.logical_not(has_next))
    def _():
        for p in range(pieces):
            spectra[p, rows + 1] = jnp.zeros((groups, cf, PW), BF16)

    def blend_row(p, i):
        for g in range(groups):
            total = None
            for j in range(4):
                at = map_ref[j, i * groups + g] * PW
                term = tables[p][:, pl.ds(at, PW)].astype(F32) * weight_ref[j, i * groups + g]
                total = term if total is None else total + term
            blended[i, g] = total.astype(BF16)

    def map_row(p, i):
        flat = blended[i].reshape(groups * cf, PW)
        products = jnp.dot(flat, stacked[...], preferred_element_type=F32)
        for g in range(groups):
            label = jnp.full((1, PW), label_ref[i * groups + g], jnp.int32)
            block = products[g * cf:(g + 1) * cf]
            picked = block[:, :PW]
            for kind in range(1, kinds):
                picked = jnp.where(label == kind, block[:, kind * PW:(kind + 1) * PW], picked)
            spectra[p, i + 1, g] = picked.astype(BF16)

    def stress_row(p, i, at):
        here = spectra[p, i + 1].astype(F32)
        from_left = pltpu.roll(here, 1, 2)
        from_right = pltpu.roll(here, PW - 1, 2)
        left = jnp.where(lane == 0, jnp.concatenate([empty, from_left[:-1]], 0), from_left)
        right = jnp.where(
            lane == PW - 1, jnp.concatenate([from_right[1:], empty], 0), from_right)
        beside = spectra[p, i].astype(F32) + spectra[p, i + 2].astype(F32) + left + right
        load[:, p, at] = (here + bending[:, i][:, None, :] * (4.0 * here - beside)).astype(BF16)

    def inner_stress(p, i):
        stress_row(p, i, i - 1)

    def edge_rows(p):
        @pl.when(has_prev)
        def _():
            down_copy(p).wait_recv()

        @pl.when(has_next)
        def _():
            up_copy(p).wait_recv()

        stress_row(p, 0, rows - 2)
        stress_row(p, rows - 1, rows - 1)

    def each(first, last, act, p, unroll):
        def body(i, carry):
            act(p, i)
            return carry
        lax.fori_loop(first, last, body, 0, unroll=unroll)

    for p in range(pieces):
        own_copy(p).wait()

        @pl.when(has_prev)
        def _():
            pressure_copy(p).wait_recv()

        for act in (blend_row, map_row):
            act(p, 0)
            act(p, rows - 1)

        @pl.when(has_prev)
        def _():
            up_copy(p).start()

        @pl.when(has_next)
        def _():
            down_copy(p).start()

        for n in range(len(cuts[p]) - 1):
            low, high = cuts[p][n], cuts[p][n + 1]
            first = low + (n > 0)
            last = min(high + 1, rows - 1)
            each(first, last, blend_row, p, 2)
            each(first, last, map_row, p, 3)
            if p == 0 and n == 0:
                for k in range(1, owners):
                    stiff_copy(k, source(k)).wait_recv()
                bending[...] = stiffs[...].astype(F32)
            each(low, high, inner_stress, p, 2)
            for k in far_first:
                column_copy(p, n, k, me).start()

        @pl.when(has_next)
        def _():
            pressure_copy(p).wait_send()
            if p + 1 < pieces:
                pressure_copy(p + 1).start()

    for n, values in enumerate(
            fourier_factors(NT, factors.shape[1], factors.shape[2] // 2, cf * pieces // 2, pieces == 2)):
        factors[n] = values

    def table_rows(n, carry):
        values = (factors[0, pl.ds(n, 1)] * factors[2] - factors[1, pl.ds(n, 1)] * factors[3])
        table[n] = values.astype(BF16)
        return carry

    lax.fori_loop(0, factors.shape[1], table_rows, 0)

    late = pieces - 1
    for p in range(pieces):
        edge_rows(p)
    for k in far_first:
        edge_copy(k, me).start()
    keep_copy().start()

    def history_rows(q, lines):
        sides = []
        for at in range(len(lines)):
            stack = [arrived[:, p, q + at].reshape(-1, PW) for p in range(pieces)]
            sides.append(stack[0] if pieces == 1 else jnp.concatenate(stack, 0))
        sides = jnp.concatenate(sides, 1)
        depth = sides.shape[0]
        per = 2 * BLOCK // table.shape[1]
        for n in range(NT // (2 * BLOCK)):
            part = table[n * per:(n + 1) * per].reshape(2 * BLOCK, depth)
            values = jnp.dot(part, sides, preferred_element_type=F32)
            for h in range(2):
                for at, line in enumerate(lines):
                    wide_ref[2 * n + h, pl.ds(line, BLOCK, stride=rows + 1), :] = (
                        values[h * BLOCK:(h + 1) * BLOCK, at * PW:(at + 1) * PW])

    def wait_columns(p, n):
        for k in range(1, owners):
            column_copy(p, n, k, source(k)).wait_recv()

    keep_copy().wait()
    for p, n in sent:
        if p < late:
            wait_columns(p, n)
    for n in range(len(cuts[late]) - 1):
        wait_columns(late, n)
        low, high = cuts[late][n], cuts[late][n + 1]
        whole = (high - low) // DEEP

        def deep_rows(m, carry):
            q = low - 1 + DEEP * m
            history_rows(q, [q + 1 + at for at in range(DEEP)])
            return carry

        lax.fori_loop(0, whole, deep_rows, 0)
        rest = low + whole * DEEP
        if rest < high:
            history_rows(rest - 1, list(range(rest, high)))
    for k in range(1, owners):
        edge_copy(k, source(k)).wait_recv()
    history_rows(rows - 2, [0, rows - 1])

    @pl.when(has_next)
    def _():
        for p in range(pieces):
            down_copy(p).wait_send()

    @pl.when(has_prev)
    def _():
        for p in range(pieces):
            up_copy(p).wait_send()

    for k in range(1, owners):
        stiff_copy(k, me).wait_send()
        for p, n in sent:
            column_copy(p, n, k, me).wait_send()
        edge_copy(k, me).wait_send()


def exchange(panel_map, weights, labels, own, templates, stiffness, groups, owners, patches):
    rows = stiffness.shape[0]
    pieces, cf, width = own.shape
    kinds = templates.shape[0]
    depth = owners * pieces * cf
    fine = math.isqrt(NT)
    smem = pl.BlockSpec(memory_space=pltpu.SMEM)
    hbm = pl.BlockSpec(memory_space=pl.ANY)
    vmem = pl.BlockSpec(memory_space=pltpu.VMEM)
    dma = pltpu.SemaphoreType.DMA
    return pl.pallas_call(
        functools.partial(exchange_kernel, rows, groups, owners, patches),
        out_shape=pltpu.VMEM((NT // BLOCK, BLOCK * (rows + 1), PW), F32),
        in_specs=[smem, smem, smem, hbm, vmem, vmem],
        out_specs=vmem,
        scratch_shapes=[
            pltpu.VMEM((rows, groups, cf, PW), BF16),
            pltpu.VMEM((pieces, rows + 2, groups, cf, PW), BF16),
            pltpu.VMEM((groups, pieces, rows, cf, PW), BF16),
            pltpu.VMEM((owners, pieces, rows, cf, PW), BF16),
            pltpu.VMEM((rows, PW), BF16),
            pltpu.VMEM((owners, rows, PW), BF16),
            pltpu.VMEM((owners, rows, PW), F32),
            pltpu.VMEM((PW, kinds * PW), BF16),
            pltpu.VMEM((4, fine, depth), F32),
            pltpu.VMEM((fine, fine, depth), BF16),
            dma((pieces + 1,)),
            dma((2, pieces)),
            dma((2, pieces, 2)),
            dma((2, owners)),
            dma((2, (pieces - 1) * (len(FIRST_SHARES) - 1) + len(LAST_SHARES), owners)),
        ] + [pltpu.VMEM((cf, 2 * width), BF16)] * pieces,
        compiler_params=pltpu.CompilerParams(
            vmem_limit_bytes=VMEM_LIMIT, collective_id=0, has_side_effects=True),
        cost_estimate=pl.CostEstimate(
            flops=2 * own.size * kinds * PW + 2 * NT * depth * rows * PW,
            bytes_accessed=40 * own.size, transcendentals=0),
    )(panel_map, weights, labels, own, templates, stiffness)


def finish_kernel(scale, gain_ref, zone_ref, wide_ref, out_ref, staged, sem):
    rows = zone_ref.shape[0]
    gain = jnp.zeros(zone_ref.shape, F32)
    for zone in range(gain_ref.shape[0]):
        gain = jnp.where(zone_ref[...] == zone, gain_ref[zone], gain)
    gain = gain * scale
    blocks = NT // BLOCK

    def write(n):
        part = pl.ds(n * BLOCK, BLOCK)
        return pltpu.make_async_copy(staged.at[part], out_ref.at[part], sem.at[n])

    for n in range(blocks):
        for t in range(BLOCK):
            values = wide_ref[n, pl.ds(t * (rows + 1), rows), :]
            staged[n * BLOCK + t] = (values * gain).astype(BF16)
        write(n).start()
    for n in range(blocks):
        write(n).wait()


def finish(wide, zone_gain, zone_ids, scale):
    rows = zone_ids.shape[0]
    return pl.pallas_call(
        functools.partial(finish_kernel, scale),
        out_shape=jax.ShapeDtypeStruct((NT, rows, PW), BF16),
        in_specs=[pl.BlockSpec(memory_space=pltpu.SMEM), pl.BlockSpec(memory_space=pltpu.VMEM),
                  pl.BlockSpec(memory_space=pltpu.VMEM)],
        out_specs=pl.BlockSpec(memory_space=pl.ANY),
        scratch_shapes=[pltpu.VMEM((NT, rows, PW), BF16), pltpu.SemaphoreType.DMA((NT // BLOCK,))],
        compiler_params=pltpu.CompilerParams(vmem_limit_bytes=FINISH_LIMIT),
        cost_estimate=pl.CostEstimate(
            flops=NT * rows * PW, bytes_accessed=2 * NT * rows * PW, transcendentals=0),
    )(zone_gain, zone_ids, pltpu.with_memory_space_constraint(wide, pltpu.VMEM))


def shards(
    pressures, templates, panel_map, blend_weights, pattern_label, zone_ids, zone_gain, stiffness
):
    owners = lax.axis_size("freq")
    fl = pressures.shape[1]
    nfreq = fl * owners
    rows, cols = zone_ids.shape
    groups = owners * cols // PW

    pieces = 2 if fl % 16 == 0 else 1
    own = pressures.reshape(pieces, 2 * fl // pieces, pressures.shape[2])
    wide = exchange(
        panel_map.T, blend_weights.T, pattern_label, own, templates, stiffness, groups, owners,
        lax.axis_size("patch"))
    return finish(wide, zone_gain, zone_ids, 1.0 / math.sqrt(nfreq))


def solution(mesh):
    placed = (
        P(None, "freq", "patch"),
        P(),
        P("patch", None),
        P("patch", None),
        P("patch"),
        P("patch", "freq"),
        P(),
        P("patch", "freq"),
    )
    return jax.shard_map(
        shards, mesh=mesh, in_specs=placed, out_specs=P(None, "patch", "freq"), check_vma=False
    )
```

```python
import functools
import math

import jax
import jax.numpy as jnp
from jax import lax
from jax.experimental import pallas as pl
from jax.experimental.pallas import tpu as pltpu
from jax.sharding import PartitionSpec as P

NT = 1024
PW = 128
BLOCK = 128
DEEP = 8
FIRST_SHARES = (0, 1, 3, 7, 15)
LAST_SHARES = (0, 7, 15)
VMEM_LIMIT = 40 * 1024 * 1024
FINISH_LIMIT = 16 * 1024 * 1024
BF16 = jnp.bfloat16
F32 = jnp.float32


def row_cuts(rows, shares):
    pairs = (rows - 2) // 2
    return [1 + 2 * (pairs * share // shares[-1]) for share in shares]


def fourier_factors(nt, fine, nfreq, fl, whole):
    step = lax.broadcasted_iota(jnp.int32, (fine, 2 * nfreq), 0)
    order = lax.broadcasted_iota(jnp.int32, (fine, 2 * nfreq), 1)
    if whole:
        real, freq = order < nfreq, order % nfreq
    else:
        real, freq = order // fl % 2 == 0, order // (2 * fl) * fl + order % fl

    def angles(clock):
        turns = clock * (freq + 1) % nt
        return turns.astype(F32) * (2.0 * math.pi / nt)

    coarse, small = angles(step * fine), angles(step)
    cosine, sine = jnp.cos(coarse), jnp.sin(coarse)
    return (jnp.where(real, cosine, -sine), jnp.where(real, sine, cosine),
            jnp.cos(small), jnp.sin(small))


def exchange_kernel(rows, groups, owners, patches, map_in, weight_in, label_in, own_ref,
                    templates_in, stiff_in, wide_ref,
                    map_ref, weight_ref, label_ref, templates_ref, stiff_ref, fetch_sem,
                    blended, spectra, load, arrived, own_stiff, stiffs, bending, stacked, factors, table,
                    local_sem, press_sem, edge_sem, stiff_sem, column_sem, *tables):
    pieces, cf, width = own_ref.shape
    kinds = templates_ref.shape[0]
    me, patch = lax.axis_index("freq"), lax.axis_index("patch")
    has_prev, has_next = patch > 0, patch < patches - 1
    lane = lax.broadcasted_iota(jnp.int32, (groups, cf, PW), 2)
    empty = jnp.zeros((1, cf, PW), F32)
    cuts = [row_cuts(rows, LAST_SHARES if p == pieces - 1 else FIRST_SHARES) for p in range(pieces)]
    offsets = [sum(len(c) - 1 for c in cuts[:p]) for p in range(pieces + 1)]
    far_first = sorted(range(1, owners), key=lambda k: -min(k, owners - k))

    def partner(k):
        return lax.rem(me + k, owners)

    def source(k):
        return lax.rem(me + owners - k, owners)

    def remote(src, dst, sems, at, **device):
        return pltpu.make_async_remote_copy(
            src_ref=src, dst_ref=dst, send_sem=sems.at[(0,) + at], recv_sem=sems.at[(1,) + at],
            device_id=device, device_id_type=pl.DeviceIdType.MESH)

    def pressure_copy(p):
        return remote(own_ref.at[p], tables[p].at[:, pl.ds(0, width)], press_sem, (p,),
                      patch=patch + 1)

    def own_copy(p):
        return pltpu.make_async_copy(
            own_ref.at[p], tables[p].at[:, pl.ds(width, width)], local_sem.at[p])

    def down_copy(p):
        return remote(spectra.at[p, rows], spectra.at[p, 0], edge_sem, (p, 0), patch=patch + 1)

    def up_copy(p):
        return remote(spectra.at[p, 1], spectra.at[p, rows + 1], edge_sem, (p, 1),
                      patch=patch - 1)

    def stiff_copy(k, slot):
        return remote(own_stiff, stiffs.at[slot], stiff_sem, (k,), freq=partner(k))

    def column_copy(p, n, k, slot):
        part = pl.ds(cuts[p][n] - 1, cuts[p][n + 1] - cuts[p][n])
        return remote(load.at[partner(k), p, part], arrived.at[slot, p, part], column_sem,
                      (offsets[p] + n, k), freq=partner(k))

    def edge_copy(k, slot):
        part = pl.ds(rows - 2, 2)
        return remote(load.at[partner(k), :, part], arrived.at[slot, :, part], column_sem,
                      (offsets[pieces], k), freq=partner(k))

    sent = [(p, n) for p in range(pieces) for n in range(len(cuts[p]) - 1)]

    def keep_copy():
        return pltpu.make_async_copy(load.at[me], arrived.at[me], local_sem.at[pieces])

    barrier = pltpu.get_barrier_semaphore()
    for k in range(1, owners):
        pl.semaphore_signal(barrier, inc=1, device_id={"freq": partner(k)},
                            device_id_type=pl.DeviceIdType.MESH)

    @pl.when(has_prev)
    def _():
        pl.semaphore_signal(barrier, inc=1, device_id={"patch": patch - 1},
                            device_id_type=pl.DeviceIdType.MESH)

    @pl.when(has_next)
    def _():
        pl.semaphore_signal(barrier, inc=1, device_id={"patch": patch + 1},
                            device_id_type=pl.DeviceIdType.MESH)

    fetches = [pltpu.make_async_copy(src, dst, fetch_sem.at[n]) for n, (src, dst) in enumerate((
        (stiff_in, stiff_ref), (map_in, map_ref), (weight_in, weight_ref), (label_in, label_ref),
        (templates_in, templates_ref)))]
    for fetch in fetches:
        fetch.start()
    for p in range(pieces):
        own_copy(p).start()
    fetches[0].wait()
    own_stiff[...] = stiff_ref[...].astype(BF16)
    pl.semaphore_wait(
        barrier, owners - 1 + has_prev.astype(jnp.int32) + has_next.astype(jnp.int32))

    @pl.when(has_next)
    def _():
        pressure_copy(0).start()

    for k in range(1, owners):
        stiff_copy(k, me).start()
    stiffs[me] = own_stiff[...]
    for fetch in fetches[1:]:
        fetch.wait()
    for kind in range(kinds):
        stacked[:, kind * PW:(kind + 1) * PW] = templates_ref[kind]

    @pl.when(jnp.logical_not(has_prev))
    def _():
        for p in range(pieces):
            tables[p][:, :width] = jnp.zeros((cf, width), BF16)
            spectra[p, 0] = jnp.zeros((groups, cf, PW), BF16)

    @pl.when(jnp.logical_not(has_next))
    def _():
        for p in range(pieces):
            spectra[p, rows + 1] = jnp.zeros((groups, cf, PW), BF16)

    def blend_row(p, i):
        for g in range(groups):
            total = None
            for j in range(4):
                at = map_ref[j, i * groups + g] * PW
                term = tables[p][:, pl.ds(at, PW)].astype(F32) * weight_ref[j, i * groups + g]
                total = term if total is None else total + term
            blended[i, g] = total.astype(BF16)

    def map_row(p, i):
        flat = blended[i].reshape(groups * cf, PW)
        products = jnp.dot(flat, stacked[...], preferred_element_type=F32)
        for g in range(groups):
            label = jnp.full((1, PW), label_ref[i * groups + g], jnp.int32)
            block = products[g * cf:(g + 1) * cf]
            picked = block[:, :PW]
            for kind in range(1, kinds):
                picked = jnp.where(label == kind, block[:, kind * PW:(kind + 1) * PW], picked)
            spectra[p, i + 1, g] = picked.astype(BF16)

    def stress_row(p, i, at):
        here = spectra[p, i + 1].astype(F32)
        from_left = pltpu.roll(here, 1, 2)
        from_right = pltpu.roll(here, PW - 1, 2)
        left = jnp.where(lane == 0, jnp.concatenate([empty, from_left[:-1]], 0), from_left)
        right = jnp.where(
            lane == PW - 1, jnp.concatenate([from_right[1:], empty], 0), from_right)
        beside = spectra[p, i].astype(F32) + spectra[p, i + 2].astype(F32) + left + right
        load[:, p, at] = (here + bending[:, i][:, None, :] * (4.0 * here - beside)).astype(BF16)

    def inner_stress(p, i):
        stress_row(p, i, i - 1)

    def edge_rows(p):
        @pl.when(has_prev)
        def _():
            down_copy(p).wait_recv()

        @pl.when(has_next)
        def _():
            up_copy(p).wait_recv()

        stress_row(p, 0, rows - 2)
        stress_row(p, rows - 1, rows - 1)

    def each(first, last, act, p, unroll):
        def body(i, carry):
            act(p, i)
            return carry
        lax.fori_loop(first, last, body, 0, unroll=unroll)

    for p in range(pieces):
        own_copy(p).wait()

        @pl.when(has_prev)
        def _():
            pressure_copy(p).wait_recv()

        blend_row(p, 0)
        map_row(p, 0)
        for n in range(len(cuts[p]) - 1):
            low, high = cuts[p][n], cuts[p][n + 1]
            first = low + (n > 0)
            last = min(high + 1, rows - 1)
            each(first, last, blend_row, p, 2)
            each(first, last, map_row, p, 3)
            if p == 0 and n == 0:
                for k in range(1, owners):
                    stiff_copy(k, source(k)).wait_recv()
                bending[...] = stiffs[...].astype(F32)
            each(low, high, inner_stress, p, 2)
            for k in far_first:
                column_copy(p, n, k, me).start()
            if n == 0:
                blend_row(p, rows - 1)
                map_row(p, rows - 1)

                @pl.when(has_prev)
                def _():
                    up_copy(p).start()

                @pl.when(has_next)
                def _():
                    down_copy(p).start()


        @pl.when(has_next)
        def _():
            pressure_copy(p).wait_send()
            if p + 1 < pieces:
                pressure_copy(p + 1).start()

    for n, values in enumerate(
            fourier_factors(NT, factors.shape[1], factors.shape[2] // 2, cf * pieces // 2, pieces == 2)):
        factors[n] = values

    def table_rows(n, carry):
        values = (factors[0, pl.ds(n, 1)] * factors[2] - factors[1, pl.ds(n, 1)] * factors[3])
        table[n] = values.astype(BF16)
        return carry

    lax.fori_loop(0, factors.shape[1], table_rows, 0)

    late = pieces - 1
    for p in range(pieces):
        edge_rows(p)
    for k in far_first:
        edge_copy(k, me).start()
    keep_copy().start()

    def history_rows(q, lines):
        sides = []
        for at in range(len(lines)):
            stack = [arrived[:, p, q + at].reshape(-1, PW) for p in range(pieces)]
            sides.append(stack[0] if pieces == 1 else jnp.concatenate(stack, 0))
        sides = jnp.concatenate(sides, 1)
        depth = sides.shape[0]
        per = 2 * BLOCK // table.shape[1]
        for n in range(NT // (2 * BLOCK)):
            part = table[n * per:(n + 1) * per].reshape(2 * BLOCK, depth)
            values = jnp.dot(part, sides, preferred_element_type=F32)
            for h in range(2):
                for at, line in enumerate(lines):
                    wide_ref[2 * n + h, pl.ds(line, BLOCK, stride=rows + 1), :] = (
                        values[h * BLOCK:(h + 1) * BLOCK, at * PW:(at + 1) * PW])

    def wait_columns(p, n):
        for k in range(1, owners):
            column_copy(p, n, k, source(k)).wait_recv()

    keep_copy().wait()
    for p, n in sent:
        if p < late:
            wait_columns(p, n)
    for n in range(len(cuts[late]) - 1):
        wait_columns(late, n)
        low, high = cuts[late][n], cuts[late][n + 1]
        whole = (high - low) // DEEP

        def deep_rows(m, carry):
            q = low - 1 + DEEP * m
            history_rows(q, [q + 1 + at for at in range(DEEP)])
            return carry

        lax.fori_loop(0, whole, deep_rows, 0)
        rest = low + whole * DEEP
        if rest < high:
            history_rows(rest - 1, list(range(rest, high)))
    for k in range(1, owners):
        edge_copy(k, source(k)).wait_recv()
    history_rows(rows - 2, [0, rows - 1])

    @pl.when(has_next)
    def _():
        for p in range(pieces):
            down_copy(p).wait_send()

    @pl.when(has_prev)
    def _():
        for p in range(pieces):
            up_copy(p).wait_send()

    for k in range(1, owners):
        stiff_copy(k, me).wait_send()
        for p, n in sent:
            column_copy(p, n, k, me).wait_send()
        edge_copy(k, me).wait_send()


def exchange(panel_map, weights, labels, own, templates, stiffness, groups, owners, patches):
    rows = stiffness.shape[0]
    pieces, cf, width = own.shape
    kinds = templates.shape[0]
    depth = owners * pieces * cf
    fine = math.isqrt(NT)
    hbm = pl.BlockSpec(memory_space=pl.ANY)
    vmem = pl.BlockSpec(memory_space=pltpu.VMEM)
    dma = pltpu.SemaphoreType.DMA
    return pl.pallas_call(
        functools.partial(exchange_kernel, rows, groups, owners, patches),
        out_shape=pltpu.VMEM((NT // BLOCK, BLOCK * (rows + 1), PW), F32),
        in_specs=[hbm] * 6,
        out_specs=vmem,
        scratch_shapes=[
            pltpu.SMEM(panel_map.shape, jnp.int32),
            pltpu.SMEM(weights.shape, F32),
            pltpu.SMEM(labels.shape, jnp.int32),
            pltpu.VMEM(templates.shape, BF16),
            pltpu.VMEM(stiffness.shape, F32),
            dma((5,)),
            pltpu.VMEM((rows, groups, cf, PW), BF16),
            pltpu.VMEM((pieces, rows + 2, groups, cf, PW), BF16),
            pltpu.VMEM((groups, pieces, rows, cf, PW), BF16),
            pltpu.VMEM((owners, pieces, rows, cf, PW), BF16),
            pltpu.VMEM((rows, PW), BF16),
            pltpu.VMEM((owners, rows, PW), BF16),
            pltpu.VMEM((owners, rows, PW), F32),
            pltpu.VMEM((PW, kinds * PW), BF16),
            pltpu.VMEM((4, fine, depth), F32),
            pltpu.VMEM((fine, fine, depth), BF16),
            dma((pieces + 1,)),
            dma((2, pieces)),
            dma((2, pieces, 2)),
            dma((2, owners)),
            dma((2, (pieces - 1) * (len(FIRST_SHARES) - 1) + len(LAST_SHARES), owners)),
        ] + [pltpu.VMEM((cf, 2 * width), BF16)] * pieces,
        compiler_params=pltpu.CompilerParams(
            vmem_limit_bytes=VMEM_LIMIT, collective_id=0, has_side_effects=True),
        cost_estimate=pl.CostEstimate(
            flops=2 * own.size * kinds * PW + 2 * NT * depth * rows * PW,
            bytes_accessed=40 * own.size, transcendentals=0),
    )(panel_map, weights, labels, own, templates, stiffness)


def finish_kernel(scale, gain_ref, zone_ref, wide_ref, out_ref, staged, sem):
    rows = zone_ref.shape[0]
    gain = jnp.zeros(zone_ref.shape, F32)
    for zone in range(gain_ref.shape[0]):
        gain = jnp.where(zone_ref[...] == zone, gain_ref[zone], gain)
    gain = gain * scale
    blocks = NT // BLOCK

    def write(n):
        part = pl.ds(n * BLOCK, BLOCK)
        return pltpu.make_async_copy(staged.at[part], out_ref.at[part], sem.at[n])

    for n in range(blocks):
        for t in range(BLOCK):
            values = wide_ref[n, pl.ds(t * (rows + 1), rows), :]
            staged[n * BLOCK + t] = (values * gain).astype(BF16)
        write(n).start()
    for n in range(blocks):
        write(n).wait()


def finish(wide, zone_gain, zone_ids, scale):
    rows = zone_ids.shape[0]
    return pl.pallas_call(
        functools.partial(finish_kernel, scale),
        out_shape=jax.ShapeDtypeStruct((NT, rows, PW), BF16),
        in_specs=[pl.BlockSpec(memory_space=pltpu.SMEM), pl.BlockSpec(memory_space=pltpu.VMEM),
                  pl.BlockSpec(memory_space=pltpu.VMEM)],
        out_specs=pl.BlockSpec(memory_space=pl.ANY),
        scratch_shapes=[pltpu.VMEM((NT, rows, PW), BF16), pltpu.SemaphoreType.DMA((NT // BLOCK,))],
        compiler_params=pltpu.CompilerParams(vmem_limit_bytes=FINISH_LIMIT),
        cost_estimate=pl.CostEstimate(
            flops=NT * rows * PW, bytes_accessed=2 * NT * rows * PW, transcendentals=0),
    )(zone_gain, zone_ids, pltpu.with_memory_space_constraint(wide, pltpu.VMEM))


def shards(
    pressures, templates, panel_map, blend_weights, pattern_label, zone_ids, zone_gain, stiffness
):
    owners = lax.axis_size("freq")
    fl = pressures.shape[1]
    nfreq = fl * owners
    rows, cols = zone_ids.shape
    groups = owners * cols // PW

    pieces = 2 if fl % 16 == 0 else 1
    own = pressures.reshape(pieces, 2 * fl // pieces, pressures.shape[2])
    wide = exchange(
        panel_map.T, blend_weights.T, pattern_label, own, templates, stiffness, groups, owners,
        lax.axis_size("patch"))
    return finish(wide, zone_gain, zone_ids, 1.0 / math.sqrt(nfreq))


def solution(mesh):
    placed = (
        P(None, "freq", "patch"),
        P(),
        P("patch", None),
        P("patch", None),
        P("patch"),
        P("patch", "freq"),
        P(),
        P("patch", "freq"),
    )
    return jax.shard_map(
        shards, mesh=mesh, in_specs=placed, out_specs=P(None, "patch", "freq"), check_vma=False
    )
```

```python
import functools
import math

import jax
import jax.numpy as jnp
from jax import lax
from jax.experimental import pallas as pl
from jax.experimental.pallas import tpu as pltpu
from jax.sharding import PartitionSpec as P

NT = 1024
PW = 128
BLOCK = 128
DEEP = 8
FIRST_SHARES = (0, 1, 3, 7, 15)
LAST_SHARES = (0, 7, 15)
VMEM_LIMIT = 40 * 1024 * 1024
FINISH_LIMIT = 16 * 1024 * 1024
BF16 = jnp.bfloat16
F32 = jnp.float32


def row_cuts(rows, shares):
    pairs = (rows - 2) // 2
    return [1 + 2 * (pairs * share // shares[-1]) for share in shares]


def fourier_factors(nt, fine, nfreq, fl, whole):
    step = lax.broadcasted_iota(jnp.int32, (fine, 2 * nfreq), 0)
    order = lax.broadcasted_iota(jnp.int32, (fine, 2 * nfreq), 1)
    if whole:
        real, freq = order < nfreq, order % nfreq
    else:
        real, freq = order // fl % 2 == 0, order // (2 * fl) * fl + order % fl

    def angles(clock):
        turns = clock * (freq + 1) % nt
        return turns.astype(F32) * (2.0 * math.pi / nt)

    coarse, small = angles(step * fine), angles(step)
    cosine, sine = jnp.cos(coarse), jnp.sin(coarse)
    return (jnp.where(real, cosine, -sine), jnp.where(real, sine, cosine),
            jnp.cos(small), jnp.sin(small))


def exchange_kernel(rows, groups, owners, patches, map_in, weight_in, label_in, own_ref,
                    templates_in, stiff_in, wide_ref,
                    map_ref, weight_ref, label_ref, templates_ref, stiff_ref, fetch_sem,
                    blended, spectra, load, arrived, own_stiff, stiffs, bending, stacked, factors, table,
                    local_sem, press_sem, edge_sem, stiff_sem, column_sem, *tables):
    pieces, cf, width = own_ref.shape
    kinds = templates_ref.shape[0]
    me, patch = lax.axis_index("freq"), lax.axis_index("patch")
    has_prev, has_next = patch > 0, patch < patches - 1
    by_owner = patch < patches // 2
    lane = lax.broadcasted_iota(jnp.int32, (groups, cf, PW), 2)
    empty = jnp.zeros((1, cf, PW), F32)
    cuts = [row_cuts(rows, LAST_SHARES if p == pieces - 1 else FIRST_SHARES) for p in range(pieces)]
    offsets = [sum(len(c) - 1 for c in cuts[:p]) for p in range(pieces + 1)]
    far_first = sorted(range(1, owners), key=lambda k: -min(k, owners - k))

    def partner(k):
        return lax.rem(me + k, owners)

    def source(k):
        return lax.rem(me + owners - k, owners)

    def remote(src, dst, sems, at, **device):
        return pltpu.make_async_remote_copy(
            src_ref=src, dst_ref=dst, send_sem=sems.at[(0,) + at], recv_sem=sems.at[(1,) + at],
            device_id=device, device_id_type=pl.DeviceIdType.MESH)

    def pressure_copy(p):
        return remote(own_ref.at[p], tables[p].at[:, pl.ds(0, width)], press_sem, (p,),
                      patch=patch + 1)

    def own_copy(p):
        return pltpu.make_async_copy(
            own_ref.at[p], tables[p].at[:, pl.ds(width, width)], local_sem.at[p])

    def down_copy(p):
        return remote(spectra.at[p, rows], spectra.at[p, 0], edge_sem, (p, 0), patch=patch + 1)

    def up_copy(p):
        return remote(spectra.at[p, 1], spectra.at[p, rows + 1], edge_sem, (p, 1),
                      patch=patch - 1)

    def stiff_copy(k, slot):
        return remote(own_stiff, stiffs.at[slot], stiff_sem, (k,), freq=partner(k))

    def column_copy(p, n, k, slot):
        part = pl.ds(cuts[p][n] - 1, cuts[p][n + 1] - cuts[p][n])
        return remote(load.at[partner(k), p, part], arrived.at[slot, p, part], column_sem,
                      (offsets[p] + n, k), freq=partner(k))

    def edge_copy(k, slot):
        part = pl.ds(rows - 2, 2)
        return remote(load.at[partner(k), :, part], arrived.at[slot, :, part], column_sem,
                      (offsets[pieces], k), freq=partner(k))

    sent = [(p, n) for p in range(pieces) for n in range(len(cuts[p]) - 1)]

    def keep_copy():
        return pltpu.make_async_copy(load.at[me], arrived.at[me], local_sem.at[pieces])

    barrier = pltpu.get_barrier_semaphore()
    for k in range(1, owners):
        pl.semaphore_signal(barrier, inc=1, device_id={"freq": partner(k)},
                            device_id_type=pl.DeviceIdType.MESH)

    @pl.when(has_prev)
    def _():
        pl.semaphore_signal(barrier, inc=1, device_id={"patch": patch - 1},
                            device_id_type=pl.DeviceIdType.MESH)

    @pl.when(has_next)
    def _():
        pl.semaphore_signal(barrier, inc=1, device_id={"patch": patch + 1},
                            device_id_type=pl.DeviceIdType.MESH)

    fetches = [pltpu.make_async_copy(src, dst, fetch_sem.at[n]) for n, (src, dst) in enumerate((
        (stiff_in, stiff_ref), (map_in, map_ref), (weight_in, weight_ref), (label_in, label_ref),
        (templates_in, templates_ref)))]
    for fetch in fetches:
        fetch.start()
    for p in range(pieces):
        own_copy(p).start()
    fetches[0].wait()
    own_stiff[...] = stiff_ref[...].astype(BF16)
    pl.semaphore_wait(
        barrier, owners - 1 + has_prev.astype(jnp.int32) + has_next.astype(jnp.int32))

    @pl.when(has_next)
    def _():
        pressure_copy(0).start()

    for k in range(1, owners):
        stiff_copy(k, me).start()
    stiffs[me] = own_stiff[...]
    for fetch in fetches[1:]:
        fetch.wait()
    for kind in range(kinds):
        stacked[:, kind * PW:(kind + 1) * PW] = templates_ref[kind]

    @pl.when(jnp.logical_not(has_prev))
    def _():
        for p in range(pieces):
            tables[p][:, :width] = jnp.zeros((cf, width), BF16)
            spectra[p, 0] = jnp.zeros((groups, cf, PW), BF16)

    @pl.when(jnp.logical_not(has_next))
    def _():
        for p in range(pieces):
            spectra[p, rows + 1] = jnp.zeros((groups, cf, PW), BF16)

    def blend_row(p, i):
        for g in range(groups):
            total = None
            for j in range(4):
                at = map_ref[j, i * groups + g] * PW
                term = tables[p][:, pl.ds(at, PW)].astype(F32) * weight_ref[j, i * groups + g]
                total = term if total is None else total + term
            blended[i, g] = total.astype(BF16)

    def map_row(p, i):
        flat = blended[i].reshape(groups * cf, PW)
        products = jnp.dot(flat, stacked[...], preferred_element_type=F32)
        for g in range(groups):
            label = jnp.full((1, PW), label_ref[i * groups + g], jnp.int32)
            block = products[g * cf:(g + 1) * cf]
            picked = block[:, :PW]
            for kind in range(1, kinds):
                picked = jnp.where(label == kind, block[:, kind * PW:(kind + 1) * PW], picked)
            spectra[p, i + 1, g] = picked.astype(BF16)

    def stress_row(p, i, at):
        here = spectra[p, i + 1].astype(F32)
        from_left = pltpu.roll(here, 1, 2)
        from_right = pltpu.roll(here, PW - 1, 2)
        left = jnp.where(lane == 0, jnp.concatenate([empty, from_left[:-1]], 0), from_left)
        right = jnp.where(
            lane == PW - 1, jnp.concatenate([from_right[1:], empty], 0), from_right)
        beside = spectra[p, i].astype(F32) + spectra[p, i + 2].astype(F32) + left + right
        load[:, p, at] = (here + bending[:, i][:, None, :] * (4.0 * here - beside)).astype(BF16)

    def inner_stress(p, i):
        stress_row(p, i, i - 1)

    def edge_rows(p):
        @pl.when(has_prev)
        def _():
            down_copy(p).wait_recv()

        @pl.when(has_next)
        def _():
            up_copy(p).wait_recv()

        stress_row(p, 0, rows - 2)
        stress_row(p, rows - 1, rows - 1)

    def each(first, last, act, p, unroll):
        def body(i, carry):
            act(p, i)
            return carry
        lax.fori_loop(first, last, body, 0, unroll=unroll)

    for p in range(pieces):
        own_copy(p).wait()

        @pl.when(has_prev)
        def _():
            pressure_copy(p).wait_recv()

        blend_row(p, 0)
        map_row(p, 0)
        for n in range(len(cuts[p]) - 1):
            low, high = cuts[p][n], cuts[p][n + 1]
            first = low + (n > 0)
            last = min(high + 1, rows - 1)
            each(first, last, blend_row, p, 2)
            each(first, last, map_row, p, 3)
            if p == 0 and n == 0:
                for k in range(1, owners):
                    stiff_copy(k, source(k)).wait_recv()
                bending[...] = stiffs[...].astype(F32)
            each(low, high, inner_stress, p, 2)
            if p < pieces - 1:
                for k in far_first:
                    column_copy(p, n, k, me).start()
            else:
                @pl.when(jnp.logical_not(by_owner))
                def _():
                    for k in far_first:
                        column_copy(p, n, k, me).start()
            if n == 0:
                blend_row(p, rows - 1)
                map_row(p, rows - 1)

                @pl.when(has_prev)
                def _():
                    up_copy(p).start()

                @pl.when(has_next)
                def _():
                    down_copy(p).start()


        @pl.when(has_next)
        def _():
            pressure_copy(p).wait_send()
            if p + 1 < pieces:
                pressure_copy(p + 1).start()

    for n, values in enumerate(
            fourier_factors(NT, factors.shape[1], factors.shape[2] // 2, cf * pieces // 2, pieces == 2)):
        factors[n] = values

    def table_rows(n, carry):
        values = (factors[0, pl.ds(n, 1)] * factors[2] - factors[1, pl.ds(n, 1)] * factors[3])
        table[n] = values.astype(BF16)
        return carry

    lax.fori_loop(0, factors.shape[1], table_rows, 0)

    late = pieces - 1
    for p in range(pieces):
        edge_rows(p)

    @pl.when(by_owner)
    def _():
        for k in far_first:
            for n in range(len(cuts[late]) - 1):
                column_copy(late, n, k, me).start()
            edge_copy(k, me).start()

    @pl.when(jnp.logical_not(by_owner))
    def _():
        for k in far_first:
            edge_copy(k, me).start()

    keep_copy().start()

    def history_rows(q, lines):
        sides = []
        for at in range(len(lines)):
            stack = [arrived[:, p, q + at].reshape(-1, PW) for p in range(pieces)]
            sides.append(stack[0] if pieces == 1 else jnp.concatenate(stack, 0))
        sides = jnp.concatenate(sides, 1)
        depth = sides.shape[0]
        per = 2 * BLOCK // table.shape[1]
        for n in range(NT // (2 * BLOCK)):
            part = table[n * per:(n + 1) * per].reshape(2 * BLOCK, depth)
            values = jnp.dot(part, sides, preferred_element_type=F32)
            for h in range(2):
                for at, line in enumerate(lines):
                    wide_ref[2 * n + h, pl.ds(line, BLOCK, stride=rows + 1), :] = (
                        values[h * BLOCK:(h + 1) * BLOCK, at * PW:(at + 1) * PW])

    def wait_columns(p, n):
        for k in range(1, owners):
            column_copy(p, n, k, source(k)).wait_recv()

    keep_copy().wait()
    for p, n in sent:
        if p < late:
            wait_columns(p, n)
    for n in range(len(cuts[late]) - 1):
        wait_columns(late, n)
        low, high = cuts[late][n], cuts[late][n + 1]
        whole = (high - low) // DEEP

        def deep_rows(m, carry):
            q = low - 1 + DEEP * m
            history_rows(q, [q + 1 + at for at in range(DEEP)])
            return carry

        lax.fori_loop(0, whole, deep_rows, 0)
        rest = low + whole * DEEP
        if rest < high:
            history_rows(rest - 1, list(range(rest, high)))
    for k in range(1, owners):
        edge_copy(k, source(k)).wait_recv()
    history_rows(rows - 2, [0, rows - 1])

    @pl.when(has_next)
    def _():
        for p in range(pieces):
            down_copy(p).wait_send()

    @pl.when(has_prev)
    def _():
        for p in range(pieces):
            up_copy(p).wait_send()

    for k in range(1, owners):
        stiff_copy(k, me).wait_send()
        for p, n in sent:
            column_copy(p, n, k, me).wait_send()
        edge_copy(k, me).wait_send()


def exchange(panel_map, weights, labels, own, templates, stiffness, groups, owners, patches):
    rows = stiffness.shape[0]
    pieces, cf, width = own.shape
    kinds = templates.shape[0]
    depth = owners * pieces * cf
    fine = math.isqrt(NT)
    hbm = pl.BlockSpec(memory_space=pl.ANY)
    vmem = pl.BlockSpec(memory_space=pltpu.VMEM)
    dma = pltpu.SemaphoreType.DMA
    return pl.pallas_call(
        functools.partial(exchange_kernel, rows, groups, owners, patches),
        out_shape=pltpu.VMEM((NT // BLOCK, BLOCK * (rows + 1), PW), F32),
        in_specs=[hbm] * 6,
        out_specs=vmem,
        scratch_shapes=[
            pltpu.SMEM(panel_map.shape, jnp.int32),
            pltpu.SMEM(weights.shape, F32),
            pltpu.SMEM(labels.shape, jnp.int32),
            pltpu.VMEM(templates.shape, BF16),
            pltpu.VMEM(stiffness.shape, F32),
            dma((5,)),
            pltpu.VMEM((rows, groups, cf, PW), BF16),
            pltpu.VMEM((pieces, rows + 2, groups, cf, PW), BF16),
            pltpu.VMEM((groups, pieces, rows, cf, PW), BF16),
            pltpu.VMEM((owners, pieces, rows, cf, PW), BF16),
            pltpu.VMEM((rows, PW), BF16),
            pltpu.VMEM((owners, rows, PW), BF16),
            pltpu.VMEM((owners, rows, PW), F32),
            pltpu.VMEM((PW, kinds * PW), BF16),
            pltpu.VMEM((4, fine, depth), F32),
            pltpu.VMEM((fine, fine, depth), BF16),
            dma((pieces + 1,)),
            dma((2, pieces)),
            dma((2, pieces, 2)),
            dma((2, owners)),
            dma((2, (pieces - 1) * (len(FIRST_SHARES) - 1) + len(LAST_SHARES), owners)),
        ] + [pltpu.VMEM((cf, 2 * width), BF16)] * pieces,
        compiler_params=pltpu.CompilerParams(
            vmem_limit_bytes=VMEM_LIMIT, collective_id=0, has_side_effects=True),
        cost_estimate=pl.CostEstimate(
            flops=2 * own.size * kinds * PW + 2 * NT * depth * rows * PW,
            bytes_accessed=40 * own.size, transcendentals=0),
    )(panel_map, weights, labels, own, templates, stiffness)


def finish_kernel(scale, gain_ref, zone_ref, wide_ref, out_ref, staged, sem):
    rows = zone_ref.shape[0]
    gain = jnp.zeros(zone_ref.shape, F32)
    for zone in range(gain_ref.shape[0]):
        gain = jnp.where(zone_ref[...] == zone, gain_ref[zone], gain)
    gain = gain * scale
    def write(n):
        return pltpu.make_async_copy(
            staged.at[n], out_ref.at[pl.ds(n * BLOCK, BLOCK)], sem.at[n])

    def block(n, carry):
        for t in range(BLOCK):
            values = wide_ref[n, pl.ds(t * (rows + 1), rows), :]
            staged[n, t] = (values * gain).astype(BF16)
        write(n).start()
        return carry

    lax.fori_loop(0, NT // BLOCK, block, 0)
    for n in range(NT // BLOCK):
        write(n).wait()


def finish(wide, zone_gain, zone_ids, scale):
    rows = zone_ids.shape[0]
    return pl.pallas_call(
        functools.partial(finish_kernel, scale),
        out_shape=jax.ShapeDtypeStruct((NT, rows, PW), BF16),
        in_specs=[pl.BlockSpec(memory_space=pltpu.SMEM), pl.BlockSpec(memory_space=pltpu.VMEM),
                  pl.BlockSpec(memory_space=pltpu.VMEM)],
        out_specs=pl.BlockSpec(memory_space=pl.ANY),
        scratch_shapes=[pltpu.VMEM((NT // BLOCK, BLOCK, rows, PW), BF16), pltpu.SemaphoreType.DMA((NT // BLOCK,))],
        compiler_params=pltpu.CompilerParams(vmem_limit_bytes=FINISH_LIMIT),
        cost_estimate=pl.CostEstimate(
            flops=NT * rows * PW, bytes_accessed=2 * NT * rows * PW, transcendentals=0),
    )(zone_gain, zone_ids, pltpu.with_memory_space_constraint(wide, pltpu.VMEM))


def shards(
    pressures, templates, panel_map, blend_weights, pattern_label, zone_ids, zone_gain, stiffness
):
    owners = lax.axis_size("freq")
    fl = pressures.shape[1]
    nfreq = fl * owners
    rows, cols = zone_ids.shape
    groups = owners * cols // PW

    pieces = 2 if fl % 16 == 0 else 1
    own = pressures.reshape(pieces, 2 * fl // pieces, pressures.shape[2])
    wide = exchange(
        panel_map.T, blend_weights.T, pattern_label, own, templates, stiffness, groups, owners,
        lax.axis_size("patch"))
    return finish(wide, zone_gain, zone_ids, 1.0 / math.sqrt(nfreq))


def solution(mesh):
    placed = (
        P(None, "freq", "patch"),
        P(),
        P("patch", None),
        P("patch", None),
        P("patch"),
        P("patch", "freq"),
        P(),
        P("patch", "freq"),
    )
    return jax.shard_map(
        shards, mesh=mesh, in_specs=placed, out_specs=P(None, "patch", "freq"), check_vma=False
    )
```

```python
import functools
import math

import jax
import jax.numpy as jnp
from jax import lax
from jax.experimental import pallas as pl
from jax.experimental.pallas import tpu as pltpu
from jax.sharding import PartitionSpec as P

NT = 1024
PW = 128
BLOCK = 128
DEEP = 8
FIRST_SHARES = (0, 1, 3, 6, 10, 15)
LAST_SHARES = (0, 7, 15)
VMEM_LIMIT = 40 * 1024 * 1024
FINISH_LIMIT = 16 * 1024 * 1024
BF16 = jnp.bfloat16
F32 = jnp.float32


def row_cuts(rows, shares):
    pairs = (rows - 2) // 2
    return [1 + 2 * (pairs * share // shares[-1]) for share in shares]


def fourier_factors(nt, fine, nfreq, fl, whole):
    step = lax.broadcasted_iota(jnp.int32, (fine, 2 * nfreq), 0)
    order = lax.broadcasted_iota(jnp.int32, (fine, 2 * nfreq), 1)
    if whole:
        real, freq = order < nfreq, order % nfreq
    else:
        real, freq = order // fl % 2 == 0, order // (2 * fl) * fl + order % fl

    def angles(clock):
        turns = clock * (freq + 1) % nt
        return turns.astype(F32) * (2.0 * math.pi / nt)

    coarse, small = angles(step * fine), angles(step)
    cosine, sine = jnp.cos(coarse), jnp.sin(coarse)
    return (jnp.where(real, cosine, -sine), jnp.where(real, sine, cosine),
            jnp.cos(small), jnp.sin(small))


def exchange_kernel(rows, groups, owners, patches, map_in, weight_in, label_in, own_ref,
                    templates_in, stiff_in, wide_ref,
                    map_ref, weight_ref, label_ref, templates_ref, stiff_ref, fetch_sem,
                    blended, spectra, load, arrived, own_stiff, stiffs, bending, stacked, factors, table,
                    local_sem, press_sem, edge_sem, stiff_sem, column_sem, *tables):
    pieces, cf, width = own_ref.shape
    kinds = templates_ref.shape[0]
    me, patch = lax.axis_index("freq"), lax.axis_index("patch")
    has_prev, has_next = patch > 0, patch < patches - 1
    by_owner = patch < patches // 2
    lane = lax.broadcasted_iota(jnp.int32, (groups, cf, PW), 2)
    empty = jnp.zeros((1, cf, PW), F32)
    cuts = [row_cuts(rows, LAST_SHARES if p == pieces - 1 else FIRST_SHARES) for p in range(pieces)]
    offsets = [sum(len(c) - 1 for c in cuts[:p]) for p in range(pieces + 1)]
    far_first = sorted(range(1, owners), key=lambda k: -min(k, owners - k))

    def partner(k):
        return lax.rem(me + k, owners)

    def source(k):
        return lax.rem(me + owners - k, owners)

    def remote(src, dst, sems, at, **device):
        return pltpu.make_async_remote_copy(
            src_ref=src, dst_ref=dst, send_sem=sems.at[(0,) + at], recv_sem=sems.at[(1,) + at],
            device_id=device, device_id_type=pl.DeviceIdType.MESH)

    def pressure_copy(p):
        return remote(own_ref.at[p], tables[p].at[:, pl.ds(0, width)], press_sem, (p,),
                      patch=patch + 1)

    def own_copy(p):
        return pltpu.make_async_copy(
            own_ref.at[p], tables[p].at[:, pl.ds(width, width)], local_sem.at[p])

    def down_copy(p):
        return remote(spectra.at[p, rows], spectra.at[p, 0], edge_sem, (p, 0), patch=patch + 1)

    def up_copy(p):
        return remote(spectra.at[p, 1], spectra.at[p, rows + 1], edge_sem, (p, 1),
                      patch=patch - 1)

    def stiff_copy(k, slot):
        return remote(own_stiff, stiffs.at[slot], stiff_sem, (k,), freq=partner(k))

    def column_copy(p, n, k, slot):
        part = pl.ds(cuts[p][n] - 1, cuts[p][n + 1] - cuts[p][n])
        return remote(load.at[partner(k), p, part], arrived.at[slot, p, part], column_sem,
                      (offsets[p] + n, k), freq=partner(k))

    def edge_copy(k, slot):
        part = pl.ds(rows - 2, 2)
        return remote(load.at[partner(k), :, part], arrived.at[slot, :, part], column_sem,
                      (offsets[pieces], k), freq=partner(k))

    sent = [(p, n) for p in range(pieces) for n in range(len(cuts[p]) - 1)]

    def keep_copy():
        return pltpu.make_async_copy(load.at[me], arrived.at[me], local_sem.at[pieces])

    barrier = pltpu.get_barrier_semaphore()
    for k in range(1, owners):
        pl.semaphore_signal(barrier, inc=1, device_id={"freq": partner(k)},
                            device_id_type=pl.DeviceIdType.MESH)

    @pl.when(has_prev)
    def _():
        pl.semaphore_signal(barrier, inc=1, device_id={"patch": patch - 1},
                            device_id_type=pl.DeviceIdType.MESH)

    @pl.when(has_next)
    def _():
        pl.semaphore_signal(barrier, inc=1, device_id={"patch": patch + 1},
                            device_id_type=pl.DeviceIdType.MESH)

    fetches = [pltpu.make_async_copy(src, dst, fetch_sem.at[n]) for n, (src, dst) in enumerate((
        (stiff_in, stiff_ref), (map_in, map_ref), (weight_in, weight_ref), (label_in, label_ref),
        (templates_in, templates_ref)))]
    for fetch in fetches:
        fetch.start()
    for p in range(pieces):
        own_copy(p).start()
    fetches[0].wait()
    own_stiff[...] = stiff_ref[...].astype(BF16)
    pl.semaphore_wait(
        barrier, owners - 1 + has_prev.astype(jnp.int32) + has_next.astype(jnp.int32))

    @pl.when(has_next)
    def _():
        pressure_copy(0).start()

    for k in range(1, owners):
        stiff_copy(k, me).start()
    stiffs[me] = own_stiff[...]
    for fetch in fetches[1:]:
        fetch.wait()
    for kind in range(kinds):
        stacked[:, kind * PW:(kind + 1) * PW] = templates_ref[kind]

    @pl.when(jnp.logical_not(has_prev))
    def _():
        for p in range(pieces):
            tables[p][:, :width] = jnp.zeros((cf, width), BF16)
            spectra[p, 0] = jnp.zeros((groups, cf, PW), BF16)

    @pl.when(jnp.logical_not(has_next))
    def _():
        for p in range(pieces):
            spectra[p, rows + 1] = jnp.zeros((groups, cf, PW), BF16)

    def blend_row(p, i):
        for g in range(groups):
            total = None
            for j in range(4):
                at = map_ref[j, i * groups + g] * PW
                term = tables[p][:, pl.ds(at, PW)].astype(F32) * weight_ref[j, i * groups + g]
                total = term if total is None else total + term
            blended[i, g] = total.astype(BF16)

    def map_row(p, i):
        flat = blended[i].reshape(groups * cf, PW)
        products = jnp.dot(flat, stacked[...], preferred_element_type=F32)
        for g in range(groups):
            label = jnp.full((1, PW), label_ref[i * groups + g], jnp.int32)
            block = products[g * cf:(g + 1) * cf]
            picked = block[:, :PW]
            for kind in range(1, kinds):
                picked = jnp.where(label == kind, block[:, kind * PW:(kind + 1) * PW], picked)
            spectra[p, i + 1, g] = picked.astype(BF16)

    def stress_row(p, i, at):
        here = spectra[p, i + 1].astype(F32)
        from_left = pltpu.roll(here, 1, 2)
        from_right = pltpu.roll(here, PW - 1, 2)
        left = jnp.where(lane == 0, jnp.concatenate([empty, from_left[:-1]], 0), from_left)
        right = jnp.where(
            lane == PW - 1, jnp.concatenate([from_right[1:], empty], 0), from_right)
        beside = spectra[p, i].astype(F32) + spectra[p, i + 2].astype(F32) + left + right
        load[:, p, at] = (here + bending[:, i][:, None, :] * (4.0 * here - beside)).astype(BF16)

    def inner_stress(p, i):
        stress_row(p, i, i - 1)

    def edge_rows(p):
        @pl.when(has_prev)
        def _():
            down_copy(p).wait_recv()

        @pl.when(has_next)
        def _():
            up_copy(p).wait_recv()

        stress_row(p, 0, rows - 2)
        stress_row(p, rows - 1, rows - 1)

    def each(first, last, act, p, unroll):
        def body(i, carry):
            act(p, i)
            return carry
        lax.fori_loop(first, last, body, 0, unroll=unroll)

    for p in range(pieces):
        own_copy(p).wait()

        @pl.when(has_prev)
        def _():
            pressure_copy(p).wait_recv()

        blend_row(p, 0)
        map_row(p, 0)
        for n in range(len(cuts[p]) - 1):
            low, high = cuts[p][n], cuts[p][n + 1]
            first = low + (n > 0)
            last = min(high + 1, rows - 1)
            each(first, last, blend_row, p, 2)
            each(first, last, map_row, p, 3)
            if p == 0 and n == 0:
                for k in range(1, owners):
                    stiff_copy(k, source(k)).wait_recv()
                bending[...] = stiffs[...].astype(F32)
            each(low, high, inner_stress, p, 2)
            if p < pieces - 1:
                for k in far_first:
                    column_copy(p, n, k, me).start()
            else:
                @pl.when(jnp.logical_not(by_owner))
                def _():
                    for k in far_first:
                        column_copy(p, n, k, me).start()
            if n == 0:
                blend_row(p, rows - 1)
                map_row(p, rows - 1)

                @pl.when(has_prev)
                def _():
                    up_copy(p).start()

                @pl.when(has_next)
                def _():
                    down_copy(p).start()


        @pl.when(has_next)
        def _():
            pressure_copy(p).wait_send()
            if p + 1 < pieces:
                pressure_copy(p + 1).start()

    late = pieces - 1
    for p in range(pieces):
        edge_rows(p)

    @pl.when(by_owner)
    def _():
        for k in far_first:
            for n in range(len(cuts[late]) - 1):
                column_copy(late, n, k, me).start()
            edge_copy(k, me).start()

    @pl.when(jnp.logical_not(by_owner))
    def _():
        for k in far_first:
            edge_copy(k, me).start()

    keep_copy().start()

    for n, values in enumerate(
            fourier_factors(NT, factors.shape[1], factors.shape[2] // 2, cf * pieces // 2, pieces == 2)):
        factors[n] = values

    def table_rows(n, carry):
        values = (factors[0, pl.ds(n, 1)] * factors[2] - factors[1, pl.ds(n, 1)] * factors[3])
        table[n] = values.astype(BF16)
        return carry

    lax.fori_loop(0, factors.shape[1], table_rows, 0)


    def history_rows(q, lines):
        sides = []
        for at in range(len(lines)):
            stack = [arrived[:, p, q + at].reshape(-1, PW) for p in range(pieces)]
            sides.append(stack[0] if pieces == 1 else jnp.concatenate(stack, 0))
        sides = jnp.concatenate(sides, 1)
        depth = sides.shape[0]
        per = 2 * BLOCK // table.shape[1]
        for n in range(NT // (2 * BLOCK)):
            part = table[n * per:(n + 1) * per].reshape(2 * BLOCK, depth)
            values = jnp.dot(part, sides, preferred_element_type=F32)
            for h in range(2):
                for at, line in enumerate(lines):
                    wide_ref[2 * n + h, pl.ds(line, BLOCK, stride=rows + 1), :] = (
                        values[h * BLOCK:(h + 1) * BLOCK, at * PW:(at + 1) * PW])

    def wait_columns(p, n):
        for k in range(1, owners):
            column_copy(p, n, k, source(k)).wait_recv()

    keep_copy().wait()
    for p, n in sent:
        if p < late:
            wait_columns(p, n)
    for n in range(len(cuts[late]) - 1):
        wait_columns(late, n)
        low, high = cuts[late][n], cuts[late][n + 1]
        whole = (high - low) // DEEP

        def deep_rows(m, carry):
            q = low - 1 + DEEP * m
            history_rows(q, [q + 1 + at for at in range(DEEP)])
            return carry

        lax.fori_loop(0, whole, deep_rows, 0)
        rest = low + whole * DEEP
        if rest < high:
            history_rows(rest - 1, list(range(rest, high)))
    for k in range(1, owners):
        edge_copy(k, source(k)).wait_recv()
    history_rows(rows - 2, [0, rows - 1])

    @pl.when(has_next)
    def _():
        for p in range(pieces):
            down_copy(p).wait_send()

    @pl.when(has_prev)
    def _():
        for p in range(pieces):
            up_copy(p).wait_send()

    for k in range(1, owners):
        stiff_copy(k, me).wait_send()
        for p, n in sent:
            column_copy(p, n, k, me).wait_send()
        edge_copy(k, me).wait_send()


def exchange(panel_map, weights, labels, own, templates, stiffness, groups, owners, patches):
    rows = stiffness.shape[0]
    pieces, cf, width = own.shape
    kinds = templates.shape[0]
    depth = owners * pieces * cf
    fine = math.isqrt(NT)
    hbm = pl.BlockSpec(memory_space=pl.ANY)
    vmem = pl.BlockSpec(memory_space=pltpu.VMEM)
    dma = pltpu.SemaphoreType.DMA
    return pl.pallas_call(
        functools.partial(exchange_kernel, rows, groups, owners, patches),
        out_shape=pltpu.VMEM((NT // BLOCK, (BLOCK + 1) * (rows + 1), PW), F32),
        in_specs=[hbm] * 6,
        out_specs=vmem,
        scratch_shapes=[
            pltpu.SMEM(panel_map.shape, jnp.int32),
            pltpu.SMEM(weights.shape, F32),
            pltpu.SMEM(labels.shape, jnp.int32),
            pltpu.VMEM(templates.shape, BF16),
            pltpu.VMEM(stiffness.shape, F32),
            dma((5,)),
            pltpu.VMEM((rows, groups, cf, PW), BF16),
            pltpu.VMEM((pieces, rows + 2, groups, cf, PW), BF16),
            pltpu.VMEM((groups, pieces, rows, cf, PW), BF16),
            pltpu.VMEM((owners, pieces, rows, cf, PW), BF16),
            pltpu.VMEM((rows, PW), BF16),
            pltpu.VMEM((owners, rows, PW), BF16),
            pltpu.VMEM((owners, rows, PW), F32),
            pltpu.VMEM((PW, kinds * PW), BF16),
            pltpu.VMEM((4, fine, depth), F32),
            pltpu.VMEM((fine, fine, depth), BF16),
            dma((pieces + 1,)),
            dma((2, pieces)),
            dma((2, pieces, 2)),
            dma((2, owners)),
            dma((2, (pieces - 1) * (len(FIRST_SHARES) - 1) + len(LAST_SHARES), owners)),
        ] + [pltpu.VMEM((cf, 2 * width), BF16)] * pieces,
        compiler_params=pltpu.CompilerParams(
            vmem_limit_bytes=VMEM_LIMIT, collective_id=0, has_side_effects=True),
        cost_estimate=pl.CostEstimate(
            flops=2 * own.size * kinds * PW + 2 * NT * depth * rows * PW,
            bytes_accessed=40 * own.size, transcendentals=0),
    )(panel_map, weights, labels, own, templates, stiffness)


def finish_kernel(scale, gain_ref, zone_ref, wide_ref, out_ref, staged, sem):
    rows = zone_ref.shape[0]
    gain = jnp.zeros(zone_ref.shape, F32)
    for zone in range(gain_ref.shape[0]):
        gain = jnp.where(zone_ref[...] == zone, gain_ref[zone], gain)
    gain = gain * scale
    def write(n):
        return pltpu.make_async_copy(
            staged.at[n], out_ref.at[pl.ds(n * BLOCK, BLOCK)], sem.at[n])

    def block(n, carry):
        for t in range(BLOCK):
            values = wide_ref[n, pl.ds(t * (rows + 1), rows), :]
            staged[n, t] = (values * gain).astype(BF16)
        write(n).start()
        return carry

    lax.fori_loop(0, NT // BLOCK, block, 0)
    for n in range(NT // BLOCK):
        write(n).wait()


def finish(wide, zone_gain, zone_ids, scale):
    rows = zone_ids.shape[0]
    return pl.pallas_call(
        functools.partial(finish_kernel, scale),
        out_shape=jax.ShapeDtypeStruct((NT, rows, PW), BF16),
        in_specs=[pl.BlockSpec(memory_space=pltpu.SMEM), pl.BlockSpec(memory_space=pltpu.VMEM),
                  pl.BlockSpec(memory_space=pltpu.VMEM)],
        out_specs=pl.BlockSpec(memory_space=pl.ANY),
        scratch_shapes=[pltpu.VMEM((NT // BLOCK, BLOCK, rows, PW), BF16), pltpu.SemaphoreType.DMA((NT // BLOCK,))],
        compiler_params=pltpu.CompilerParams(vmem_limit_bytes=FINISH_LIMIT),
        cost_estimate=pl.CostEstimate(
            flops=NT * rows * PW, bytes_accessed=2 * NT * rows * PW, transcendentals=0),
    )(zone_gain, zone_ids, pltpu.with_memory_space_constraint(wide, pltpu.VMEM))


def shards(
    pressures, templates, panel_map, blend_weights, pattern_label, zone_ids, zone_gain, stiffness
):
    owners = lax.axis_size("freq")
    fl = pressures.shape[1]
    nfreq = fl * owners
    rows, cols = zone_ids.shape
    groups = owners * cols // PW

    pieces = 2 if fl % 16 == 0 else 1
    own = pressures.reshape(pieces, 2 * fl // pieces, pressures.shape[2])
    wide = exchange(
        panel_map.T, blend_weights.T, pattern_label, own, templates, stiffness, groups, owners,
        lax.axis_size("patch"))
    return finish(wide, zone_gain, zone_ids, 1.0 / math.sqrt(nfreq))


def solution(mesh):
    placed = (
        P(None, "freq", "patch"),
        P(),
        P("patch", None),
        P("patch", None),
        P("patch"),
        P("patch", "freq"),
        P(),
        P("patch", "freq"),
    )
    return jax.shard_map(
        shards, mesh=mesh, in_specs=placed, out_specs=P(None, "patch", "freq"), check_vma=False
    )
```

```python
import functools
import math

import jax
import jax.numpy as jnp
from jax import lax
from jax.experimental import pallas as pl
from jax.experimental.pallas import tpu as pltpu
from jax.sharding import PartitionSpec as P

NT = 1024
PW = 128
BLOCK = 128
DEEP = 8
FIRST_SHARES = (0, 1, 3, 6, 10, 15)
LAST_SHARES = (0, 7, 15)
VMEM_LIMIT = 40 * 1024 * 1024
FINISH_LIMIT = 16 * 1024 * 1024
BF16 = jnp.bfloat16
F32 = jnp.float32


def row_cuts(rows, shares):
    pairs = (rows - 2) // 2
    return [1 + 2 * (pairs * share // shares[-1]) for share in shares]


def fourier_factors(nt, fine, nfreq, fl, whole):
    step = lax.broadcasted_iota(jnp.int32, (fine, 2 * nfreq), 0)
    order = lax.broadcasted_iota(jnp.int32, (fine, 2 * nfreq), 1)
    if whole:
        real, freq = order < nfreq, order % nfreq
    else:
        real, freq = order // fl % 2 == 0, order // (2 * fl) * fl + order % fl

    def angles(clock):
        turns = clock * (freq + 1) % nt
        return turns.astype(F32) * (2.0 * math.pi / nt)

    coarse, small = angles(step * fine), angles(step)
    cosine, sine = jnp.cos(coarse), jnp.sin(coarse)
    return (jnp.where(real, cosine, -sine), jnp.where(real, sine, cosine),
            jnp.cos(small), jnp.sin(small))


def exchange_kernel(rows, groups, owners, patches, scale, map_in, weight_in, label_in, own_ref,
                    templates_in, stiff_in, zone_in, gain_in, wide_ref, field_ref,
                    map_ref, weight_ref, label_ref, templates_ref, stiff_ref, zone_ref, gain_ref, fetch_sem,
                    blended, spectra, load, arrived, own_stiff, stiffs, bending, stacked, factors, table,
                    local_sem, press_sem, edge_sem, stiff_sem, column_sem, *tables):
    pieces, cf, width = own_ref.shape
    kinds = templates_ref.shape[0]
    me, patch = lax.axis_index("freq"), lax.axis_index("patch")
    has_prev, has_next = patch > 0, patch < patches - 1
    by_owner = patch < patches // 2
    lane = lax.broadcasted_iota(jnp.int32, (groups, cf, PW), 2)
    empty = jnp.zeros((1, cf, PW), F32)
    cuts = [row_cuts(rows, LAST_SHARES if p == pieces - 1 else FIRST_SHARES) for p in range(pieces)]
    offsets = [sum(len(c) - 1 for c in cuts[:p]) for p in range(pieces + 1)]
    far_first = sorted(range(1, owners), key=lambda k: -min(k, owners - k))

    def partner(k):
        return lax.rem(me + k, owners)

    def source(k):
        return lax.rem(me + owners - k, owners)

    def remote(src, dst, sems, at, **device):
        return pltpu.make_async_remote_copy(
            src_ref=src, dst_ref=dst, send_sem=sems.at[(0,) + at], recv_sem=sems.at[(1,) + at],
            device_id=device, device_id_type=pl.DeviceIdType.MESH)

    def pressure_copy(p):
        return remote(own_ref.at[p], tables[p].at[:, pl.ds(0, width)], press_sem, (p,),
                      patch=patch + 1)

    def own_copy(p):
        return pltpu.make_async_copy(
            own_ref.at[p], tables[p].at[:, pl.ds(width, width)], local_sem.at[p])

    def down_copy(p):
        return remote(spectra.at[p, rows], spectra.at[p, 0], edge_sem, (p, 0), patch=patch + 1)

    def up_copy(p):
        return remote(spectra.at[p, 1], spectra.at[p, rows + 1], edge_sem, (p, 1),
                      patch=patch - 1)

    def stiff_copy(k, slot):
        return remote(own_stiff, stiffs.at[slot], stiff_sem, (k,), freq=partner(k))

    def column_copy(p, n, k, slot):
        part = pl.ds(cuts[p][n] - 1, cuts[p][n + 1] - cuts[p][n])
        return remote(load.at[partner(k), p, part], arrived.at[slot, p, part], column_sem,
                      (offsets[p] + n, k), freq=partner(k))

    def edge_copy(k, slot):
        part = pl.ds(rows - 2, 2)
        return remote(load.at[partner(k), :, part], arrived.at[slot, :, part], column_sem,
                      (offsets[pieces], k), freq=partner(k))

    sent = [(p, n) for p in range(pieces) for n in range(len(cuts[p]) - 1)]

    def keep_copy():
        return pltpu.make_async_copy(load.at[me], arrived.at[me], local_sem.at[pieces])

    barrier = pltpu.get_barrier_semaphore()
    for k in range(1, owners):
        pl.semaphore_signal(barrier, inc=1, device_id={"freq": partner(k)},
                            device_id_type=pl.DeviceIdType.MESH)

    @pl.when(has_prev)
    def _():
        pl.semaphore_signal(barrier, inc=1, device_id={"patch": patch - 1},
                            device_id_type=pl.DeviceIdType.MESH)

    @pl.when(has_next)
    def _():
        pl.semaphore_signal(barrier, inc=1, device_id={"patch": patch + 1},
                            device_id_type=pl.DeviceIdType.MESH)

    fetches = [pltpu.make_async_copy(src, dst, fetch_sem.at[n]) for n, (src, dst) in enumerate((
        (stiff_in, stiff_ref), (map_in, map_ref), (weight_in, weight_ref), (label_in, label_ref),
        (templates_in, templates_ref), (zone_in, zone_ref), (gain_in, gain_ref)))]
    for fetch in fetches:
        fetch.start()
    for p in range(pieces):
        own_copy(p).start()
    fetches[0].wait()
    own_stiff[...] = stiff_ref[...].astype(BF16)
    pl.semaphore_wait(
        barrier, owners - 1 + has_prev.astype(jnp.int32) + has_next.astype(jnp.int32))

    @pl.when(has_next)
    def _():
        pressure_copy(0).start()

    for k in range(1, owners):
        stiff_copy(k, me).start()
    stiffs[me] = own_stiff[...]
    for fetch in fetches[1:]:
        fetch.wait()
    for kind in range(kinds):
        stacked[:, kind * PW:(kind + 1) * PW] = templates_ref[kind]

    @pl.when(jnp.logical_not(has_prev))
    def _():
        for p in range(pieces):
            tables[p][:, :width] = jnp.zeros((cf, width), BF16)
            spectra[p, 0] = jnp.zeros((groups, cf, PW), BF16)

    @pl.when(jnp.logical_not(has_next))
    def _():
        for p in range(pieces):
            spectra[p, rows + 1] = jnp.zeros((groups, cf, PW), BF16)

    def blend_row(p, i):
        for g in range(groups):
            total = None
            for j in range(4):
                at = map_ref[j, i * groups + g] * PW
                term = tables[p][:, pl.ds(at, PW)].astype(F32) * weight_ref[j, i * groups + g]
                total = term if total is None else total + term
            blended[i, g] = total.astype(BF16)

    def map_row(p, i):
        flat = blended[i].reshape(groups * cf, PW)
        products = jnp.dot(flat, stacked[...], preferred_element_type=F32)
        for g in range(groups):
            label = jnp.full((1, PW), label_ref[i * groups + g], jnp.int32)
            block = products[g * cf:(g + 1) * cf]
            picked = block[:, :PW]
            for kind in range(1, kinds):
                picked = jnp.where(label == kind, block[:, kind * PW:(kind + 1) * PW], picked)
            spectra[p, i + 1, g] = picked.astype(BF16)

    def stress_row(p, i, at):
        here = spectra[p, i + 1].astype(F32)
        from_left = pltpu.roll(here, 1, 2)
        from_right = pltpu.roll(here, PW - 1, 2)
        left = jnp.where(lane == 0, jnp.concatenate([empty, from_left[:-1]], 0), from_left)
        right = jnp.where(
            lane == PW - 1, jnp.concatenate([from_right[1:], empty], 0), from_right)
        beside = spectra[p, i].astype(F32) + spectra[p, i + 2].astype(F32) + left + right
        load[:, p, at] = (here + bending[:, i][:, None, :] * (4.0 * here - beside)).astype(BF16)

    def inner_stress(p, i):
        stress_row(p, i, i - 1)

    def edge_rows(p):
        @pl.when(has_prev)
        def _():
            down_copy(p).wait_recv()

        @pl.when(has_next)
        def _():
            up_copy(p).wait_recv()

        stress_row(p, 0, rows - 2)
        stress_row(p, rows - 1, rows - 1)

    def each(first, last, act, p, unroll):
        def body(i, carry):
            act(p, i)
            return carry
        lax.fori_loop(first, last, body, 0, unroll=unroll)

    for p in range(pieces):
        own_copy(p).wait()

        @pl.when(has_prev)
        def _():
            pressure_copy(p).wait_recv()

        blend_row(p, 0)
        map_row(p, 0)
        for n in range(len(cuts[p]) - 1):
            low, high = cuts[p][n], cuts[p][n + 1]
            first = low + (n > 0)
            last = min(high + 1, rows - 1)
            each(first, last, blend_row, p, 2)
            each(first, last, map_row, p, 3)
            if p == 0 and n == 0:
                for k in range(1, owners):
                    stiff_copy(k, source(k)).wait_recv()
                bending[...] = stiffs[...].astype(F32)
            each(low, high, inner_stress, p, 2)
            if p < pieces - 1:
                for k in far_first:
                    column_copy(p, n, k, me).start()
            else:
                @pl.when(jnp.logical_not(by_owner))
                def _():
                    for k in far_first:
                        column_copy(p, n, k, me).start()
            if n == 0:
                blend_row(p, rows - 1)
                map_row(p, rows - 1)

                @pl.when(has_prev)
                def _():
                    up_copy(p).start()

                @pl.when(has_next)
                def _():
                    down_copy(p).start()


        @pl.when(has_next)
        def _():
            pressure_copy(p).wait_send()
            if p + 1 < pieces:
                pressure_copy(p + 1).start()

    late = pieces - 1
    for p in range(pieces):
        edge_rows(p)

    @pl.when(by_owner)
    def _():
        for k in far_first:
            for n in range(len(cuts[late]) - 1):
                column_copy(late, n, k, me).start()
            edge_copy(k, me).start()

    @pl.when(jnp.logical_not(by_owner))
    def _():
        for k in far_first:
            edge_copy(k, me).start()

    keep_copy().start()

    gain = jnp.zeros(zone_ref.shape, F32)
    for zone in range(gain_ref.shape[0]):
        gain = jnp.where(zone_ref[...] == zone, gain_ref[zone], gain)
    field_ref[...] = gain * scale

    for n, values in enumerate(
            fourier_factors(NT, factors.shape[1], factors.shape[2] // 2, cf * pieces // 2, pieces == 2)):
        factors[n] = values

    def table_rows(n, carry):
        values = (factors[0, pl.ds(n, 1)] * factors[2] - factors[1, pl.ds(n, 1)] * factors[3])
        table[n] = values.astype(BF16)
        return carry

    lax.fori_loop(0, factors.shape[1], table_rows, 0)


    def history_rows(q, lines):
        sides = []
        for at in range(len(lines)):
            stack = [arrived[:, p, q + at].reshape(-1, PW) for p in range(pieces)]
            sides.append(stack[0] if pieces == 1 else jnp.concatenate(stack, 0))
        sides = jnp.concatenate(sides, 1)
        depth = sides.shape[0]
        per = 2 * BLOCK // table.shape[1]
        for n in range(NT // (2 * BLOCK)):
            part = table[n * per:(n + 1) * per].reshape(2 * BLOCK, depth)
            values = jnp.dot(part, sides, preferred_element_type=F32)
            for h in range(2):
                for at, line in enumerate(lines):
                    wide_ref[2 * n + h, pl.ds(line, BLOCK, stride=rows + 1), :] = (
                        values[h * BLOCK:(h + 1) * BLOCK, at * PW:(at + 1) * PW])

    def wait_columns(p, n):
        for k in range(1, owners):
            column_copy(p, n, k, source(k)).wait_recv()

    keep_copy().wait()
    for p, n in sent:
        if p < late:
            wait_columns(p, n)
    for n in range(len(cuts[late]) - 1):
        wait_columns(late, n)
        low, high = cuts[late][n], cuts[late][n + 1]
        whole = (high - low) // DEEP

        def deep_rows(m, carry):
            q = low - 1 + DEEP * m
            history_rows(q, [q + 1 + at for at in range(DEEP)])
            return carry

        lax.fori_loop(0, whole, deep_rows, 0)
        rest = low + whole * DEEP
        if rest < high:
            history_rows(rest - 1, list(range(rest, high)))
    for k in range(1, owners):
        edge_copy(k, source(k)).wait_recv()
    history_rows(rows - 2, [0, rows - 1])

    @pl.when(has_next)
    def _():
        for p in range(pieces):
            down_copy(p).wait_send()

    @pl.when(has_prev)
    def _():
        for p in range(pieces):
            up_copy(p).wait_send()

    for k in range(1, owners):
        stiff_copy(k, me).wait_send()
        for p, n in sent:
            column_copy(p, n, k, me).wait_send()
        edge_copy(k, me).wait_send()


def exchange(panel_map, weights, labels, own, templates, stiffness, zone_ids, zone_gain, scale, groups, owners, patches):
    rows = stiffness.shape[0]
    pieces, cf, width = own.shape
    kinds = templates.shape[0]
    depth = owners * pieces * cf
    fine = math.isqrt(NT)
    hbm = pl.BlockSpec(memory_space=pl.ANY)
    vmem = pl.BlockSpec(memory_space=pltpu.VMEM)
    dma = pltpu.SemaphoreType.DMA
    return pl.pallas_call(
        functools.partial(exchange_kernel, rows, groups, owners, patches, scale),
        out_shape=(pltpu.VMEM((NT // BLOCK, (BLOCK + 1) * (rows + 1), PW), F32),
                   pltpu.VMEM((rows, PW), F32)),
        in_specs=[hbm] * 8,
        out_specs=(vmem, vmem),
        scratch_shapes=[
            pltpu.SMEM(panel_map.shape, jnp.int32),
            pltpu.SMEM(weights.shape, F32),
            pltpu.SMEM(labels.shape, jnp.int32),
            pltpu.VMEM(templates.shape, BF16),
            pltpu.VMEM(stiffness.shape, F32),
            pltpu.VMEM(zone_ids.shape, jnp.int32),
            pltpu.SMEM(zone_gain.shape, F32),
            dma((7,)),
            pltpu.VMEM((rows, groups, cf, PW), BF16),
            pltpu.VMEM((pieces, rows + 2, groups, cf, PW), BF16),
            pltpu.VMEM((groups, pieces, rows, cf, PW), BF16),
            pltpu.VMEM((owners, pieces, rows, cf, PW), BF16),
            pltpu.VMEM((rows, PW), BF16),
            pltpu.VMEM((owners, rows, PW), BF16),
            pltpu.VMEM((owners, rows, PW), F32),
            pltpu.VMEM((PW, kinds * PW), BF16),
            pltpu.VMEM((4, fine, depth), F32),
            pltpu.VMEM((fine, fine, depth), BF16),
            dma((pieces + 1,)),
            dma((2, pieces)),
            dma((2, pieces, 2)),
            dma((2, owners)),
            dma((2, (pieces - 1) * (len(FIRST_SHARES) - 1) + len(LAST_SHARES), owners)),
        ] + [pltpu.VMEM((cf, 2 * width), BF16)] * pieces,
        compiler_params=pltpu.CompilerParams(
            vmem_limit_bytes=VMEM_LIMIT, collective_id=0, has_side_effects=True),
        cost_estimate=pl.CostEstimate(
            flops=2 * own.size * kinds * PW + 2 * NT * depth * rows * PW,
            bytes_accessed=40 * own.size, transcendentals=0),
    )(panel_map, weights, labels, own, templates, stiffness, zone_ids, zone_gain)


def finish_kernel(field_ref, wide_ref, out_ref, staged, sem):
    rows = field_ref.shape[0]
    gain = field_ref[...]

    def write(n):
        return pltpu.make_async_copy(
            staged.at[n], out_ref.at[pl.ds(n * BLOCK, BLOCK)], sem.at[n])

    def block(n, carry):
        for t in range(BLOCK):
            values = wide_ref[n, pl.ds(t * (rows + 1), rows), :]
            staged[n, t] = (values * gain).astype(BF16)
        write(n).start()
        return carry

    lax.fori_loop(0, NT // BLOCK, block, 0)
    for n in range(NT // BLOCK):
        write(n).wait()


def finish(wide, field):
    rows = field.shape[0]
    return pl.pallas_call(
        finish_kernel,
        out_shape=jax.ShapeDtypeStruct((NT, rows, PW), BF16),
        in_specs=[pl.BlockSpec(memory_space=pltpu.VMEM)] * 2,
        out_specs=pl.BlockSpec(memory_space=pl.ANY),
        scratch_shapes=[pltpu.VMEM((NT // BLOCK, BLOCK, rows, PW), BF16), pltpu.SemaphoreType.DMA((NT // BLOCK,))],
        compiler_params=pltpu.CompilerParams(vmem_limit_bytes=FINISH_LIMIT),
        cost_estimate=pl.CostEstimate(
            flops=NT * rows * PW, bytes_accessed=2 * NT * rows * PW, transcendentals=0),
    )(*(pltpu.with_memory_space_constraint(x, pltpu.VMEM) for x in (field, wide)))


def shards(
    pressures, templates, panel_map, blend_weights, pattern_label, zone_ids, zone_gain, stiffness
):
    owners = lax.axis_size("freq")
    fl = pressures.shape[1]
    nfreq = fl * owners
    rows, cols = zone_ids.shape
    groups = owners * cols // PW

    pieces = 2 if fl % 16 == 0 else 1
    own = pressures.reshape(pieces, 2 * fl // pieces, pressures.shape[2])
    wide, field = exchange(
        panel_map.T, blend_weights.T, pattern_label, own, templates, stiffness, zone_ids, zone_gain,
        1.0 / math.sqrt(nfreq), groups, owners, lax.axis_size("patch"))
    return finish(wide, field)


def solution(mesh):
    placed = (
        P(None, "freq", "patch"),
        P(),
        P("patch", None),
        P("patch", None),
        P("patch"),
        P("patch", "freq"),
        P(),
        P("patch", "freq"),
    )
    return jax.shard_map(
        shards, mesh=mesh, in_specs=placed, out_specs=P(None, "patch", "freq"), check_vma=False
    )
```
